32 devices in a mesh: dp: 16 (over z, y, x), mp: 2 (over core).
Axes of the slice: x: 2, y: 2, z: 4, core: 2. Of those that a mesh axis runs over, the one named last changes fastest.
Arguments:
- preact: float32 [16, 16, 16, 1024], P('dp', None, None, 'mp'), may hold values from -6 to 6
- weights: float32 [512, 9, 1024], P('mp'), may hold values from -0.0625 to 0.0625
- cotangent: float32 [16, 16, 16, 512], P('dp', None, None, 'mp'), may hold values from -24 to 24
Outputs:
- output: float32 [16, 16, 16, 512], P('dp', None, None, 'mp')
- input_grad: float32 [16, 16, 16, 1024], P('dp', None, None, 'mp')
- weight_grad: float32 [512, 9216], P('mp', 'dp')
The draws below stay inside these ranges and needn't reach their ends.
All inputs are finite; a program needn't handle non-finite values.
Results may differ from the reference program's by a relative error of at most 0.0003.
Values sent between devices are 32-bit elements; how exact they have to be, the bound alone decides.
No kernel may reach another device: no remote copies, remote signals or barrier semaphores. Data moves between devices by JAX's collectives and lax.ppermute only.
A program may use at most 64 MiB of HBM per device.

```python
import jax
import jax.numpy as jnp
from jax import lax

CIN = 1024
COUT = 512
SIDE = 16
IMG_DEV = 1
IMAGES = 16
N_DP = 16


def draw_cotangent(key, part):
    shared = jax.random.normal(jax.random.fold_in(key, 101), (SIDE, SIDE, COUT), jnp.float32)
    progress = jnp.arange(IMAGES, dtype=jnp.float32) / max(IMAGES - 1, 1)
    jitter = jax.random.uniform(jax.random.fold_in(key, 103), (IMAGES,), jnp.float32, 0.8, 1.25)
    channel_scale = jnp.exp(jax.random.uniform(jax.random.fold_in(key, 104), (COUT,), jnp.float32, -1.2, 1.2))
    fluctuation = jax.random.normal(jax.random.fold_in(key, 102), (IMAGES, SIDE, SIDE, COUT), jnp.float32)
    image_scale = 3.0 ** progress * jitter
    drawn = image_scale[:, None, None, None] * channel_scale * (0.7 * shared + 0.7 * fluctuation)
    return jnp.clip(drawn, -24.0, 24.0)


def block_scale(stream_key, dims, split, least, largest):
    def one(axis_at, blocks):
        draws = jax.random.uniform(jax.random.fold_in(jax.random.fold_in(stream_key, 6), axis_at), (blocks,), jnp.float32, least / len(split), largest / len(split))
        return jnp.repeat(jnp.exp(draws), dims[axis_at] // blocks).reshape((-1,) + (1,) * (len(dims) - axis_at - 1))

    loudness = one(*split[0])
    for cut in split[1:]:
        loudness = loudness * one(*cut)
    return loudness


def gaussian(own_key, dims, scale, bound, shards=(), kind=jnp.bfloat16):
    factor_of = block_scale(own_key, dims, shards, -0.22, 0.18) if shards else 1.0
    array = jax.random.normal(own_key, dims, jnp.float32) * scale * factor_of
    return jnp.minimum(jnp.maximum(array, -bound), bound).astype(kind)


def setup_inputs(seed: int = 0) -> dict:
    streams_of = jax.random.split(jax.random.key(seed), 4)
    return {
        "preact": gaussian(streams_of[0], (IMAGES, SIDE, SIDE, CIN), 1.0, 6.0, ((0, 16), (3, 2)), jnp.float32),
        "weights": gaussian(streams_of[1], (COUT, 9, CIN), (9 * CIN) ** -0.5, 0.0625, ((0, 2),), jnp.float32),
        "cotangent": draw_cotangent(jax.random.fold_in(streams_of[3], 71), 0),
    }


highest = lax.Precision.HIGHEST
epsilon = 1e-06

def activate(values):
    return 0.5 * values * (1.0 + lax.erf(values * 0.7071067811865476))

def gelu_slope(values):
    return 0.5 * (1.0 + lax.erf(values * 0.7071067811865476)) + values * jnp.exp(-0.5 * values * values) * 0.3989422804014327

def convolve(activity, filters):
    kernel = filters.reshape(filters.shape[0], 3, 3, filters.shape[2]).transpose(1, 2, 3, 0)
    return lax.conv_general_dilated(activity, kernel, (1, 1), 'SAME', dimension_numbers=('NHWC', 'HWIO', 'NHWC'), precision=highest)

def adasum(leading, second):
    cross = jnp.sum(leading * second)
    lead_sq = jnp.sum(leading * leading)
    second_sq = jnp.sum(second * second)
    return (1.0 - cross / (2.0 * (lead_sq + epsilon))) * leading + (1.0 - cross / (2.0 * (second_sq + epsilon))) * second

def reference(preact, weights, cotangent):
    activated = activate(preact)
    output = convolve(activated, weights)
    unused, pullback = jax.vjp(lambda activity: convolve(activity, weights), activated)
    input_grad = pullback(cotangent)[0] * gelu_slope(preact)

    def leaf_grad(position):
        begin = (position * IMG_DEV).astype(jnp.int32)
        activity = lax.dynamic_slice_in_dim(activated, begin, IMG_DEV, 0)
        upstream = lax.dynamic_slice_in_dim(cotangent, begin, IMG_DEV, 0)
        unused_out, pull_leaf = jax.vjp(lambda filters: convolve(activity, filters), weights)
        return pull_leaf(upstream)[0] / float(IMG_DEV * SIDE * SIDE)

    def pair_grad(position):
        return adasum(leaf_grad(2 * position), leaf_grad(2 * position + 1))
    stacked = lax.map(pair_grad, jnp.arange(N_DP // 2, dtype=jnp.int32))
    while stacked.shape[0] > 1:
        halves = stacked.reshape((stacked.shape[0] // 2, 2) + stacked.shape[1:])
        stacked = jax.vmap(adasum)(halves[:, 0], halves[:, 1])
    weight_grad = stacked[0].reshape(COUT, 9 * CIN)
    return (output, input_grad, weight_grad)
```

```python
import functools

import jax
import jax.numpy as jnp
from jax import lax
from jax.experimental import pallas as pl
from jax.experimental.pallas import tpu as pltpu
from jax.sharding import PartitionSpec as P

highest = lax.Precision.HIGHEST
epsilon = 1e-06
MIB = 1 << 20


def from_partner(x, axis, apart):
    return lax.ppermute(x, axis, [(i, i ^ 1 << apart) for i in range(lax.axis_size(axis))])


def activate(values):
    return 0.5 * values * (1.0 + lax.erf(values * 0.7071067811865476))


def gelu_slope(values):
    return (
        0.5 * (1.0 + lax.erf(values * 0.7071067811865476))
        + values * jnp.exp(-0.5 * values * values) * 0.3989422804014327
    )


def pad_image(values):
    return jnp.pad(values, ((0, 0), (1, 1), (1, 1), (0, 0)))


def convolve_piece(activity, filters):
    extent = activity.shape[1]
    padded = pad_image(activity)
    summed = jnp.zeros(activity.shape[:3] + (filters.shape[0],), jnp.float32)
    for kernel_tap in range(9):
        row_shift, column_shift = divmod(kernel_tap, 3)
        window = padded[:, row_shift : row_shift + extent, column_shift : column_shift + extent, :]
        summed = summed + jnp.einsum(
            "nhwc,oc->nhwo", window, filters[:, kernel_tap, :], precision=highest
        )
    return summed


def weight_piece(activity, upstream):
    extent = activity.shape[1]
    padded = pad_image(activity)
    tap_grads = []
    for kernel_tap in range(9):
        row_shift, column_shift = divmod(kernel_tap, 3)
        window = padded[:, row_shift : row_shift + extent, column_shift : column_shift + extent, :]
        tap_grads.append(jnp.einsum("nhwo,nhwc->oc", upstream, window, precision=highest))
    return jnp.stack(tap_grads, 1)


def input_partial(upstream, filters):
    extent = upstream.shape[1]
    padded = pad_image(upstream)
    summed = jnp.zeros(upstream.shape[:3] + (filters.shape[2],), jnp.float32)
    for kernel_tap in range(9):
        row_shift, column_shift = divmod(kernel_tap, 3)
        window = padded[
            :,
            2 - row_shift : 2 - row_shift + extent,
            2 - column_shift : 2 - column_shift + extent,
            :,
        ]
        summed = summed + jnp.einsum(
            "nhwo,oc->nhwc", window, filters[:, kernel_tap, :], precision=highest
        )
    return summed


def adasum_halving(gradient):
    filter_count = gradient.shape[0]
    groups = lax.axis_size("dp")
    height = groups.bit_length() - 1
    data_index = lax.axis_index("dp")
    breadth = gradient.shape[1] * gradient.shape[2] // groups
    current = gradient.reshape(filter_count, groups, breadth)
    for section in range(height):
        parity = data_index >> section & 1
        paired = current.reshape(filter_count, current.shape[1] // 2, 2, breadth)
        kept_rows = lax.dynamic_slice_in_dim(paired, parity, 1, 2)[:, :, 0]
        sent_rows = lax.dynamic_slice_in_dim(paired, 1 - parity, 1, 2)[:, :, 0]
        partner = from_partner(sent_rows, "dp", section)
        lower = parity == 0
        leading = jnp.where(lower, kept_rows, partner)
        second = jnp.where(lower, partner, kept_rows)
        moments = jnp.stack(
            [jnp.sum(leading * second), jnp.sum(leading * leading), jnp.sum(second * second)]
        )
        for bit_level in range(section + 1):
            moments = moments + from_partner(moments, "dp", bit_level)
        moments = lax.psum(moments, "mp")
        cross = moments[0]
        lead_sq = moments[1]
        second_sq = moments[2]
        current = (1.0 - cross / (2.0 * (lead_sq + epsilon))) * leading + (
            1.0 - cross / (2.0 * (second_sq + epsilon))
        ) * second
    return current.reshape(filter_count, breadth)


def local_any(preact, weights, cotangent):
    activity = activate(preact)
    positions = preact.shape[0] * preact.shape[1] * preact.shape[2]
    output = convolve_piece(lax.all_gather(activity, "mp", axis=3, tiled=True), weights)
    gradient = weight_piece(lax.all_gather(activity, "mp", axis=3, tiled=True), cotangent)
    partial_sum = input_partial(cotangent, weights)
    input_grad = lax.psum_scatter(partial_sum, "mp", scatter_dimension=3, tiled=True) * gelu_slope(
        preact
    )
    weight_grad = adasum_halving(gradient / float(positions))
    return (output, input_grad, weight_grad)


VMEM = pl.BlockSpec(memory_space=pltpu.VMEM)
SMEM = pl.BlockSpec(memory_space=pltpu.SMEM)


def params(limit):
    return pltpu.CompilerParams(vmem_limit_bytes=limit * MIB)


def split(values):
    high = values.astype(jnp.bfloat16)
    low = (values - high.astype(jnp.float32)).astype(jnp.bfloat16)
    return high, low


def dot(left, right, contract):
    return lax.dot_general(
        left, right, (contract, ((), ())), preferred_element_type=jnp.float32
    )


def dot3(left, right, contract):
    lh, ll = left
    rh, rl = right
    return dot(lh, rh, contract) + (dot(lh, rl, contract) + dot(ll, rh, contract))


def shifted(values, offset, extent):
    if offset == 0:
        return values
    rows = values.shape[0]
    column = lax.rem(lax.broadcasted_iota(jnp.int32, values.shape, 0), extent)
    if offset == 1:
        moved = jnp.concatenate([values[rows - 1 :], values[: rows - 1]], 0)
        return jnp.where(column >= 1, moved, 0.0)
    moved = jnp.concatenate([values[1:], values[:1]], 0)
    return jnp.where(column < extent - 1, moved, 0.0)


def aligned(index, size):
    return pl.ds(pl.multiple_of(index * size, size), size)


def prepare_kernel(where_ref, preact_ref, up_ref, act_ref, *message_refs):
    act_ref[...] = activate(preact_ref[...])
    member = where_ref[0]
    channels = message_refs[0].shape[2]
    for other, message in enumerate(message_refs):
        target = member ^ other
        message[0] = act_ref[:, aligned(target >> 1, channels)]
        message[1] = up_ref[:, aligned(target & 1, channels)]


def image_kernel(extent, where_ref, mine_ref, theirs_ref, up_ref, weight_ref,
                 out_ref, keep_ref, send_ref,
                 act_high, act_low, up_high, up_low, total, back):
    step = pl.program_id(0)
    pixels, channels = mine_ref.shape
    core = where_ref[1]

    @pl.when(step == 0)
    def _():
        for ref in (act_high, act_low):
            ref[...] = jnp.zeros_like(ref)
        for part, place in ((mine_ref, core), (theirs_ref, 1 - core)):
            high, low = split(part[...])
            act_high[extent : extent + pixels, aligned(place, channels)] = high
            act_low[extent : extent + pixels, aligned(place, channels)] = low
        for ref in (up_high, up_low):
            ref[...] = jnp.zeros_like(ref)
        for column in range(3):
            high, low = split(shifted(up_ref[...], column - 1, extent))
            up_high[column, extent : extent + pixels] = high
            up_low[column, extent : extent + pixels] = low
        total[...] = jnp.zeros_like(total)
        back[...] = jnp.zeros_like(back)

    row, column = step // 3, lax.rem(step, 3)
    weight = split(weight_ref[0])
    window = pl.ds(pl.multiple_of(row * extent, extent), pixels)
    total[column] += dot3((act_high[window, :], act_low[window, :]), weight, ((1,), (1,)))
    window = pl.ds(pl.multiple_of((2 - row) * extent, extent), pixels)
    back[...] += dot3((up_high[column, window], up_low[column, window]), weight, ((1,), (0,)))

    @pl.when(step == pl.num_programs(0) - 1)
    def _():
        out_ref[...] = (
            shifted(total[0], 1, extent) + total[1] + shifted(total[2], -1, extent)
        )
        keep_ref[...] = back[:, aligned(core, channels)]
        send_ref[...] = back[:, aligned(1 - core, channels)]


def pairs(count):
    return [(i, j) for i in range(count) for j in range(i, count)]


def leaf_kernel(extent, images, where_ref, *refs):
    messages, swapped = refs[:images], refs[images : 2 * images]
    leaf_out, gram_ref = refs[2 * images : 2 * images + 2]
    left, right, leaf, sems = refs[2 * images + 2 :]
    pixels, filters = messages[0].shape[1:]
    member, core = where_ref[0], where_ref[1]
    scale = 1.0 / pixels
    channels = filters

    for other in range(images):
        for part, place in ((messages[other][0], core), (swapped[other][...], 1 - core)):
            high, low = split(part.T)
            rows = aligned(place, channels)
            left[other, rows, 0:pixels] = high
            left[other, rows, pixels : 2 * pixels] = high
            left[other, rows, 2 * pixels : 3 * pixels] = low
        for column in range(3):
            moved = shifted(messages[other][1] * scale, column - 1, extent)
            for row in range(3):
                tap = 3 * row + column
                gap = jnp.zeros((extent, filters), jnp.float32)
                if row == 0:
                    placed = jnp.concatenate([moved[extent:], gap], 0)
                elif row == 2:
                    placed = jnp.concatenate([gap, moved[: pixels - extent]], 0)
                else:
                    placed = moved
                high, low = split(placed)
                lanes = slice(tap * filters, (tap + 1) * filters)
                right[other, 0:pixels, lanes] = high
                right[other, pixels : 2 * pixels, lanes] = low
                right[other, 2 * pixels : 3 * pixels, lanes] = high

    def one(other, carry):
        image = member ^ other
        product = dot(left[other], right[other], ((1,), (0,)))
        depth = 2 * channels
        for tap in range(9):
            leaf[image, tap * depth : (tap + 1) * depth, :] = product[
                :, tap * filters : (tap + 1) * filters
            ]
        pltpu.make_async_copy(leaf.at[image], leaf_out.at[image], sems.at[other]).start()
        return carry

    lax.fori_loop(0, images, one, 0)

    def add(chunk, sums):
        rows = pl.ds(pl.multiple_of(chunk * 8, 8), 8)
        blocks = [leaf[i, rows, :] for i in range(images)]
        return tuple(s + blocks[i] * blocks[j] for s, (i, j) in zip(sums, pairs(images)))

    zero = jnp.zeros((8, filters), jnp.float32)
    sums = lax.fori_loop(0, leaf.shape[1] // 8, add, tuple(zero for _ in pairs(images)))
    gram_ref[...] = jnp.zeros_like(gram_ref)
    for at, block in enumerate(sums):
        gram_ref[at : at + 1, :] = jnp.sum(block, 0, keepdims=True)
    for other in range(images):
        pltpu.make_async_copy(
            leaf.at[member ^ other], leaf_out.at[member ^ other], sems.at[other]
        ).wait()


def factors(cross, lead_sq, second_sq):
    return (
        1.0 - cross / (2.0 * (lead_sq + epsilon)),
        1.0 - cross / (2.0 * (second_sq + epsilon)),
    )


def tree_factors(gram, images):
    inner = {pair: gram[at : at + 1, :] for at, pair in enumerate(pairs(images))}
    held = [1.0] * images
    count, width = images, 1
    while count > 1:
        scaled = []
        for node in range(0, count, 2):
            scaled += factors(
                inner[node, node + 1],
                jnp.maximum(inner[node, node], 0.0),
                jnp.maximum(inner[node + 1, node + 1], 0.0),
            )
        held = [value * scaled[at // width] for at, value in enumerate(held)]
        merged = {}
        for i, j in pairs(count // 2):
            terms = [
                scaled[2 * i + u] * scaled[2 * j + v] * inner[min(2 * i + u, 2 * j + v), max(2 * i + u, 2 * j + v)]
                for u in range(2)
                for v in range(2)
            ]
            merged[i, j] = (terms[0] + terms[1]) + (terms[2] + terms[3])
        inner, count, width = merged, count // 2, 2 * width
    return held


def combine_kernel(images, where_ref, gram_ref, leaf_ref, out_ref):
    gram = jnp.sum(gram_ref[...], 1, keepdims=True)
    held = tree_factors(gram, images)
    total = held[0] * leaf_ref[0]
    for image in range(1, images):
        total = total + held[image] * leaf_ref[image]
    out_ref[...] = total


def first_unit(target, part):
    low = 2 * part
    return jnp.where(low >= target, 2 * target, jnp.where(low + 1 >= target, 2 * target + 1, 2 * target + 2))


def pack(member, source_ref, message_refs, unit, start):
    for other, message in enumerate(message_refs):
        target = member ^ other
        first = first_unit(target, member >> 1)
        rows = message.shape[0] - start
        message[start:, :] = source_ref[pl.ds(pl.multiple_of(first * unit, unit), rows), :]


def pack_kernel(unit, where_ref, own_ref, *message_refs):
    pack(where_ref[0], own_ref, message_refs, unit, 0)


def moments_kernel(unit, where_ref, own_ref, far_ref, *message_refs):
    pack(where_ref[0], far_ref, message_refs, unit, 8)
    lower = where_ref[2] == 0
    own, far = own_ref[...], far_ref[...]
    cross = jnp.sum(own * far, 0, keepdims=True)
    own_sq = jnp.sum(own * own, 0, keepdims=True)
    far_sq = jnp.sum(far * far, 0, keepdims=True)
    lead_sq = jnp.where(lower, own_sq, far_sq)
    second_sq = jnp.where(lower, far_sq, own_sq)
    rest = jnp.zeros((5, own.shape[1]), jnp.float32)
    block = jnp.concatenate([cross, lead_sq, second_sq, rest], 0)
    for message in message_refs:
        message[0:8, :] = block


def finish_kernel(unit, images, where_ref, moments_ref, *refs):
    own, far = refs[:images], refs[images : 2 * images]
    out_ref, placed, turned = refs[2 * images :]
    member, lower = where_ref[0], where_ref[2] == 0
    moments = jnp.sum(moments_ref[...], 1, keepdims=True)
    lead, second = factors(moments[0:1], moments[1:2], moments[2:3])
    own_factor = jnp.where(lower, lead, second)
    far_factor = jnp.where(lower, second, lead)
    filters = own[0].shape[1]
    for other in range(images):
        rows = own[other].shape[0]
        placed[member ^ other, 0:rows, :] = own_factor * own[other][...] + far_factor * far[other][8:, :]
    for place in range(images + 1):
        kind = (member + place) & (images - 1)
        part = kind >> 1
        at = jnp.where(
            part == member >> 1, 0 if place == 0 else 2 if place == images else 1, kind & 1
        )
        rows = pl.ds(pl.multiple_of(at * unit, unit), unit)
        for half in range(2):
            turned[place * unit : (place + 1) * unit, half * filters : (half + 1) * filters] = placed[
                2 * part + half, rows, :
            ]
    out_ref[...] = turned[...].T


def exchange(x, other):
    size = lax.axis_size("dp")
    return lax.ppermute(x, "dp", [(i, i ^ other) for i in range(size)])


def swap_cores(x):
    return lax.ppermute(x, "mp", [(0, 1), (1, 0)])


def f32(*shape):
    return jax.ShapeDtypeStruct(shape, jnp.float32)


def local_cube(preact, weights, cotangent):
    extent, own_channels = preact.shape[2], preact.shape[3]
    pixels = preact.shape[1] * preact.shape[2]
    filters, taps, channels = weights.shape
    images = taps - 1
    lanes = own_channels // 4
    unit = channels // lax.axis_size("dp")
    depth = 2 * lanes * taps
    half = depth // 2
    data_index = lax.axis_index("dp")
    where = jnp.stack([data_index & (images - 1), lax.axis_index("mp"), data_index // images]).astype(jnp.int32)

    before = preact.reshape(pixels, own_channels)
    upstream = cotangent.reshape(pixels, filters)
    activity, *sent = pl.pallas_call(
        prepare_kernel,
        in_specs=[SMEM, VMEM, VMEM],
        out_specs=[VMEM] * (1 + images),
        out_shape=[f32(pixels, own_channels)] + [f32(2, pixels, lanes)] * images,
        compiler_params=params(32),
        name="prepare",
    )(where, before, upstream)
    messages = [sent[0]] + [exchange(sent[other], other) for other in range(1, images)]

    theirs = swap_cores(activity)
    tap_weights = weights.transpose(1, 0, 2)
    output, kept, given = pl.pallas_call(
        functools.partial(image_kernel, extent),
        grid=(taps,),
        in_specs=[SMEM, VMEM, VMEM, VMEM, pl.BlockSpec((1, filters, channels), lambda t: (t, 0, 0))],
        out_specs=[VMEM] * 3,
        out_shape=[f32(pixels, filters), f32(pixels, own_channels), f32(pixels, own_channels)],
        scratch_shapes=[
            pltpu.VMEM((pixels + 2 * extent, channels), jnp.bfloat16),
            pltpu.VMEM((pixels + 2 * extent, channels), jnp.bfloat16),
            pltpu.VMEM((3, pixels + 2 * extent, filters), jnp.bfloat16),
            pltpu.VMEM((3, pixels + 2 * extent, filters), jnp.bfloat16),
            pltpu.VMEM((3, pixels, filters), jnp.float32),
            pltpu.VMEM((pixels, channels), jnp.float32),
        ],
        compiler_params=params(40),
        cost_estimate=pl.CostEstimate(
            flops=12 * pixels * filters * taps * channels,
            bytes_accessed=4 * filters * taps * channels,
            transcendentals=0,
        ),
        name="image",
    )(where, activity, theirs, upstream, tap_weights)
    input_grad = (kept + swap_cores(given)) * gelu_slope(before)

    swapped = swap_cores(jnp.stack([message[0] for message in messages]))
    inner_count = len(pairs(images))
    inner_rows = -(-inner_count // 8) * 8
    leaves, gram = pl.pallas_call(
        functools.partial(leaf_kernel, extent, images),
        in_specs=[SMEM] + [VMEM] * (2 * images),
        out_specs=[pl.BlockSpec(memory_space=pl.ANY), VMEM],
        out_shape=[f32(images, depth, lanes), f32(inner_rows, lanes)],
        scratch_shapes=[
            pltpu.VMEM((images, 2 * lanes, 3 * pixels), jnp.bfloat16),
            pltpu.VMEM((images, 3 * pixels, taps * lanes), jnp.bfloat16),
            pltpu.VMEM((images, depth, lanes), jnp.float32),
            pltpu.SemaphoreType.DMA((images,)),
        ],
        compiler_params=params(48),
        name="leaf",
    )(where, *messages, *[swapped[i] for i in range(images)])
    for bit in range(3):
        gram = gram + from_partner(gram, "dp", bit)
    gram = gram + swap_cores(gram)

    def combined(which):
        step = half // 9
        return pl.pallas_call(
            functools.partial(combine_kernel, images),
            grid_spec=pltpu.PrefetchScalarGridSpec(
                num_scalar_prefetch=1,
                grid=(half // step,),
                in_specs=[
                    pl.BlockSpec((inner_rows, lanes), lambda i, at: (0, 0)),
                    pl.BlockSpec(
                        (images, step, lanes), lambda i, at: (0, at[0] * (half // step) + i, 0)
                    ),
                ],
                out_specs=pl.BlockSpec((step, lanes), lambda i, at: (i, 0)),
            ),
            out_shape=f32(half, lanes),
            compiler_params=params(32),
            name="combine",
        )(which.reshape(1), gram, leaves)

    side = where[2]
    far = exchange(combined(1 - side), images)
    own = combined(side)
    counts = [3 if other < 2 else 2 for other in range(images)]
    own_sent = pl.pallas_call(
        functools.partial(pack_kernel, unit),
        in_specs=[SMEM, VMEM],
        out_specs=[VMEM] * images,
        out_shape=[f32(count * unit, lanes) for count in counts],
        compiler_params=params(32),
        name="pack",
    )(where, own)
    own_messages = [own_sent[0]] + [exchange(own_sent[other], other) for other in range(1, images)]
    far_sent = pl.pallas_call(
        functools.partial(moments_kernel, unit),
        in_specs=[SMEM, VMEM, VMEM],
        out_specs=[VMEM] * images,
        out_shape=[f32(8 + count * unit, lanes) for count in counts],
        compiler_params=params(32),
        name="moments",
    )(where, own, far)
    far_messages = [far_sent[0]] + [exchange(far_sent[other], other) for other in range(1, images)]
    moments = functools.reduce(jnp.add, [message[0:8] for message in far_messages])
    moments = moments + swap_cores(moments)
    moments = moments + exchange(moments, images)
    weight_grad = pl.pallas_call(
        functools.partial(finish_kernel, unit, images),
        in_specs=[SMEM] + [VMEM] * (1 + 2 * images),
        out_specs=VMEM,
        out_shape=f32(filters, taps * unit),
        scratch_shapes=[
            pltpu.VMEM((images, 3 * unit, lanes), jnp.float32),
            pltpu.VMEM((taps * unit, filters), jnp.float32),
        ],
        compiler_params=params(32),
        name="finish",
    )(where, moments, *own_messages, *far_messages)
    return (
        output.reshape(cotangent.shape),
        input_grad.reshape(preact.shape),
        weight_grad,
    )


def local(preact, weights, cotangent):
    count, rows, extent, channels = preact.shape
    filters, taps = weights.shape[:2]
    fits = (
        count == 1
        and taps == 9
        and extent % 16 == 0
        and lax.axis_size("mp") == 2
        and lax.axis_size("dp") == 2 * (taps - 1)
        and channels == 4 * 128
        and filters == 2 * 128
    )
    if fits:
        return local_cube(preact, weights, cotangent)
    return local_any(preact, weights, cotangent)


def solution(mesh):
    in_specs = (P("dp", None, None, "mp"), P("mp", None, None), P("dp", None, None, "mp"))
    out_specs = (P("dp", None, None, "mp"), P("dp", None, None, "mp"), P("mp", "dp"))
    return jax.shard_map(local, mesh=mesh, in_specs=in_specs, out_specs=out_specs, check_vma=False)
```

```python
import functools

import jax
import jax.numpy as jnp
from jax import lax
from jax.experimental import pallas as pl
from jax.experimental.pallas import tpu as pltpu
from jax.sharding import PartitionSpec as P

highest = lax.Precision.HIGHEST
epsilon = 1e-06
MIB = 1 << 20


def from_partner(x, axis, apart):
    return lax.ppermute(x, axis, [(i, i ^ 1 << apart) for i in range(lax.axis_size(axis))])


def activate(values):
    return 0.5 * values * (1.0 + lax.erf(values * 0.7071067811865476))


def gelu_slope(values):
    return (
        0.5 * (1.0 + lax.erf(values * 0.7071067811865476))
        + values * jnp.exp(-0.5 * values * values) * 0.3989422804014327
    )


def pad_image(values):
    return jnp.pad(values, ((0, 0), (1, 1), (1, 1), (0, 0)))


def convolve_piece(activity, filters):
    extent = activity.shape[1]
    padded = pad_image(activity)
    summed = jnp.zeros(activity.shape[:3] + (filters.shape[0],), jnp.float32)
    for kernel_tap in range(9):
        row_shift, column_shift = divmod(kernel_tap, 3)
        window = padded[:, row_shift : row_shift + extent, column_shift : column_shift + extent, :]
        summed = summed + jnp.einsum(
            "nhwc,oc->nhwo", window, filters[:, kernel_tap, :], precision=highest
        )
    return summed


def weight_piece(activity, upstream):
    extent = activity.shape[1]
    padded = pad_image(activity)
    tap_grads = []
    for kernel_tap in range(9):
        row_shift, column_shift = divmod(kernel_tap, 3)
        window = padded[:, row_shift : row_shift + extent, column_shift : column_shift + extent, :]
        tap_grads.append(jnp.einsum("nhwo,nhwc->oc", upstream, window, precision=highest))
    return jnp.stack(tap_grads, 1)


def input_partial(upstream, filters):
    extent = upstream.shape[1]
    padded = pad_image(upstream)
    summed = jnp.zeros(upstream.shape[:3] + (filters.shape[2],), jnp.float32)
    for kernel_tap in range(9):
        row_shift, column_shift = divmod(kernel_tap, 3)
        window = padded[
            :,
            2 - row_shift : 2 - row_shift + extent,
            2 - column_shift : 2 - column_shift + extent,
            :,
        ]
        summed = summed + jnp.einsum(
            "nhwo,oc->nhwc", window, filters[:, kernel_tap, :], precision=highest
        )
    return summed


def adasum_halving(gradient):
    filter_count = gradient.shape[0]
    groups = lax.axis_size("dp")
    height = groups.bit_length() - 1
    data_index = lax.axis_index("dp")
    breadth = gradient.shape[1] * gradient.shape[2] // groups
    current = gradient.reshape(filter_count, groups, breadth)
    for section in range(height):
        parity = data_index >> section & 1
        paired = current.reshape(filter_count, current.shape[1] // 2, 2, breadth)
        kept_rows = lax.dynamic_slice_in_dim(paired, parity, 1, 2)[:, :, 0]
        sent_rows = lax.dynamic_slice_in_dim(paired, 1 - parity, 1, 2)[:, :, 0]
        partner = from_partner(sent_rows, "dp", section)
        lower = parity == 0
        leading = jnp.where(lower, kept_rows, partner)
        second = jnp.where(lower, partner, kept_rows)
        moments = jnp.stack(
            [jnp.sum(leading * second), jnp.sum(leading * leading), jnp.sum(second * second)]
        )
        for bit_level in range(section + 1):
            moments = moments + from_partner(moments, "dp", bit_level)
        moments = lax.psum(moments, "mp")
        cross = moments[0]
        lead_sq = moments[1]
        second_sq = moments[2]
        current = (1.0 - cross / (2.0 * (lead_sq + epsilon))) * leading + (
            1.0 - cross / (2.0 * (second_sq + epsilon))
        ) * second
    return current.reshape(filter_count, breadth)


def local_any(preact, weights, cotangent):
    activity = activate(preact)
    positions = preact.shape[0] * preact.shape[1] * preact.shape[2]
    output = convolve_piece(lax.all_gather(activity, "mp", axis=3, tiled=True), weights)
    gradient = weight_piece(lax.all_gather(activity, "mp", axis=3, tiled=True), cotangent)
    partial_sum = input_partial(cotangent, weights)
    input_grad = lax.psum_scatter(partial_sum, "mp", scatter_dimension=3, tiled=True) * gelu_slope(
        preact
    )
    weight_grad = adasum_halving(gradient / float(positions))
    return (output, input_grad, weight_grad)


VMEM = pl.BlockSpec(memory_space=pltpu.VMEM)


def params(limit):
    return pltpu.CompilerParams(vmem_limit_bytes=limit * MIB)


def split(values):
    high = values.astype(jnp.bfloat16)
    low = (values - high.astype(jnp.float32)).astype(jnp.bfloat16)
    return high, low


def dot(left, right, contract):
    return lax.dot_general(
        left, right, (contract, ((), ())), preferred_element_type=jnp.float32
    )


def dot3(left, right, contract):
    lh, ll = left
    rh, rl = right
    return dot(lh, rh, contract) + (dot(lh, rl, contract) + dot(ll, rh, contract))


def shifted(values, offset, extent):
    if offset == 0:
        return values
    rows = values.shape[0]
    column = lax.rem(lax.broadcasted_iota(jnp.int32, values.shape, 0), extent)
    if offset == 1:
        moved = jnp.concatenate([values[rows - 1 :], values[: rows - 1]], 0)
        return jnp.where(column >= 1, moved, 0.0)
    moved = jnp.concatenate([values[1:], values[:1]], 0)
    return jnp.where(column < extent - 1, moved, 0.0)


def aligned(index, size):
    return pl.ds(pl.multiple_of(index * size, size), size)


def place():
    index = lax.axis_index("dp")
    return index & 7, index >> 3, lax.axis_index("mp")


def prepare_kernel(preact_ref, up_ref, act_ref, *message_refs):
    act_ref[...] = activate(preact_ref[...])
    member = place()[0]
    channels = message_refs[0].shape[2]
    for other, message in enumerate(message_refs):
        target = member ^ other
        message[0] = act_ref[:, aligned(target >> 1, channels)]
        message[1] = up_ref[:, aligned(target & 1, channels)]


def image_kernel(extent, mine_ref, theirs_ref, up_ref, weight_ref,
                 out_ref, keep_ref, send_ref,
                 act_high, act_low, up_high, up_low, total, back):
    step = pl.program_id(0)
    pixels, channels = mine_ref.shape
    core = place()[2]

    @pl.when(step == 0)
    def _():
        for ref in (act_high, act_low):
            ref[...] = jnp.zeros_like(ref)
        for part, at in ((mine_ref, core), (theirs_ref, 1 - core)):
            high, low = split(part[...])
            act_high[extent : extent + pixels, aligned(at, channels)] = high
            act_low[extent : extent + pixels, aligned(at, channels)] = low
        for ref in (up_high, up_low):
            ref[...] = jnp.zeros_like(ref)
        for column in range(3):
            high, low = split(shifted(up_ref[...], column - 1, extent))
            up_high[column, extent : extent + pixels] = high
            up_low[column, extent : extent + pixels] = low
        total[...] = jnp.zeros_like(total)
        back[...] = jnp.zeros_like(back)

    row, column = step // 3, lax.rem(step, 3)
    weight = split(weight_ref[0])
    window = pl.ds(pl.multiple_of(row * extent, extent), pixels)
    total[column] += dot3((act_high[window, :], act_low[window, :]), weight, ((1,), (1,)))
    window = pl.ds(pl.multiple_of((2 - row) * extent, extent), pixels)
    back[...] += dot3((up_high[column, window], up_low[column, window]), weight, ((1,), (0,)))

    @pl.when(step == pl.num_programs(0) - 1)
    def _():
        out_ref[...] = (
            shifted(total[0], 1, extent) + total[1] + shifted(total[2], -1, extent)
        )
        keep_ref[...] = back[:, aligned(core, channels)]
        send_ref[...] = back[:, aligned(1 - core, channels)]


def pairs(count):
    return [(i, j) for i in range(count) for j in range(i, count)]


def leaf_kernel(extent, images, known, others, *refs):
    count = len(others)
    messages, swapped = refs[:count], refs[count : 2 * count]
    refs = refs[2 * count :]
    if known:
        products_in, _ = refs[:2]
        refs = refs[2:]
    leaf, products_ref, left, right = refs[:4]
    pixels, filters = messages[0].shape[1:]
    member, _, core = place()
    scale = 1.0 / pixels
    channels = filters
    depth = 2 * channels

    for at, other in enumerate(others):
        for part, where in ((messages[at][0], core), (swapped[at][...], 1 - core)):
            high, low = split(part.T)
            rows = aligned(where, channels)
            left[at, rows, 0:pixels] = high
            left[at, rows, pixels : 2 * pixels] = high
            left[at, rows, 2 * pixels : 3 * pixels] = low
        for column in range(3):
            moved = shifted(messages[at][1] * scale, column - 1, extent)
            gap = jnp.zeros((extent, filters), jnp.float32)
            for row in range(3):
                if row == 0:
                    placed = jnp.concatenate([moved[extent:], gap], 0)
                elif row == 2:
                    placed = jnp.concatenate([gap, moved[: pixels - extent]], 0)
                else:
                    placed = moved
                high, low = split(placed)
                tap = 3 * row + column
                lanes = slice(tap * filters, (tap + 1) * filters)
                right[at, 0:pixels, lanes] = high
                right[at, pixels : 2 * pixels, lanes] = low
                right[at, 2 * pixels : 3 * pixels, lanes] = high
        product = dot(left[at], right[at], ((1,), (0,)))
        image = member ^ other
        for tap in range(9):
            leaf[image, tap * depth : (tap + 1) * depth, :] = product[
                :, tap * filters : (tap + 1) * filters
            ]

    fresh = [(i, j) for at, i in enumerate(others) for j in list(known) + list(others[: at + 1])]
    held = list(known) + list(others)

    def add(chunk, sums):
        rows = pl.ds(pl.multiple_of(chunk * 8, 8), 8)
        blocks = {i: leaf[member ^ i, rows, :] for i in held}
        return tuple(s + blocks[i] * blocks[j] for s, (i, j) in zip(sums, fresh))

    zero = jnp.zeros((8, filters), jnp.float32)
    sums = lax.fori_loop(0, leaf.shape[1] // 8, add, tuple(zero for _ in fresh), unroll=4)
    table = products_ref if len(held) < images else refs[4]
    if known:
        table[...] = products_in[...]
    else:
        table[...] = jnp.zeros_like(table)
    for block, (i, j) in zip(sums, fresh):
        line = jnp.sum(block, 0, keepdims=True)
        table[i * images + j : i * images + j + 1, :] = line
        table[j * images + i : j * images + i + 1, :] = line
    if len(held) == images:
        products_ref[...] = jnp.zeros_like(products_ref)
        for at, (i, j) in enumerate(pairs(images)):
            products_ref[at : at + 1, :] = table[pl.ds((member ^ i) * images + (member ^ j), 1), :]


def factors(cross, lead_sq, second_sq):
    return (
        1.0 - cross / (2.0 * (lead_sq + epsilon)),
        1.0 - cross / (2.0 * (second_sq + epsilon)),
    )


def tree_factors(gram, images):
    inner = {pair: gram[at : at + 1, :] for at, pair in enumerate(pairs(images))}
    held = [1.0] * images
    count, width = images, 1
    while count > 1:
        scaled = []
        for node in range(0, count, 2):
            scaled += factors(
                inner[node, node + 1],
                jnp.maximum(inner[node, node], 0.0),
                jnp.maximum(inner[node + 1, node + 1], 0.0),
            )
        held = [value * scaled[at // width] for at, value in enumerate(held)]
        merged = {}
        for i, j in pairs(count // 2):
            terms = [
                scaled[2 * i + u] * scaled[2 * j + v] * inner[min(2 * i + u, 2 * j + v), max(2 * i + u, 2 * j + v)]
                for u in range(2)
                for v in range(2)
            ]
            merged[i, j] = (terms[0] + terms[1]) + (terms[2] + terms[3])
        inner, count, width = merged, count // 2, 2 * width
    return held


def combine(held, leaf_ref, start, out_ref):
    size = 64

    def some(chunk, carry):
        at = pl.multiple_of(start + chunk * size, size)
        total = held[0] * leaf_ref[0, pl.ds(at, size), :]
        for image in range(1, len(held)):
            total = total + held[image] * leaf_ref[image, pl.ds(at, size), :]
        out_ref[pl.ds(pl.multiple_of(chunk * size, size), size), :] = total
        return carry

    lax.fori_loop(0, out_ref.shape[0] // size, some, 0)


def far_kernel(gram_ref, leaf_ref, out_ref):
    images = leaf_ref.shape[0]
    held = tree_factors(jnp.sum(gram_ref[...], 1, keepdims=True), images)
    combine(held, leaf_ref, (1 - place()[1]) * out_ref.shape[0], out_ref)


def own_kernel(unit, gram_ref, leaf_ref, out_ref, *message_refs):
    images = leaf_ref.shape[0]
    member, cube, _ = place()
    held = tree_factors(jnp.sum(gram_ref[...], 1, keepdims=True), images)
    combine(held, leaf_ref, cube * out_ref.shape[0], out_ref)
    for other, message in zip(EARLY, message_refs):
        pack(member, out_ref, message, other, unit, 0)


def first_unit(target, part):
    low = 2 * part
    return jnp.where(low >= target, 2 * target, jnp.where(low + 1 >= target, 2 * target + 1, 2 * target + 2))


def units(other):
    return 3 if other < 2 else 2


def pack(member, source_ref, message, other, unit, start):
    first = first_unit(member ^ other, member >> 1)
    rows = units(other) * unit
    message[start : start + rows, :] = source_ref[pl.ds(pl.multiple_of(first * unit, unit), rows), :]


def moments_kernel(unit, own_ref, far_ref, *message_refs):
    member, cube, _ = place()
    lower = cube == 0
    own, far = own_ref[...], far_ref[...]
    cross = jnp.sum(own * far, 0, keepdims=True)
    own_sq = jnp.sum(own * own, 0, keepdims=True)
    far_sq = jnp.sum(far * far, 0, keepdims=True)
    lead_sq = jnp.where(lower, own_sq, far_sq)
    second_sq = jnp.where(lower, far_sq, own_sq)
    rest = jnp.zeros((5, own.shape[1]), jnp.float32)
    block = jnp.concatenate([cross, lead_sq, second_sq, rest], 0)
    for other, message in enumerate(message_refs):
        message[0:8, :] = block
        pack(member, far_ref, message, other, unit, 8)
        if other not in EARLY:
            pack(member, own_ref, message, other, unit, 8 + units(other) * unit)


def finish_kernel(unit, images, moments_ref, *refs):
    far, own = refs[:images], refs[images:-2]
    out_ref, placed = refs[-2:]
    member, cube, _ = place()
    lower = cube == 0
    moments = jnp.sum(moments_ref[...], 1, keepdims=True)
    lead, second = factors(moments[0:1], moments[1:2], moments[2:3])
    own_factor = jnp.where(lower, lead, second)
    far_factor = jnp.where(lower, second, lead)
    filters = placed.shape[2]
    for other in range(images):
        rows = units(other) * unit
        own_rows = own[EARLY.index(other)][...] if other in EARLY else far[other][8 + rows :, :]
        placed[member ^ other, 0:rows, :] = own_factor * own_rows + far_factor * far[other][8 : 8 + rows, :]
    for slot in range(images + 1):
        kind = (member + slot) & (images - 1)
        part = kind >> 1
        at = jnp.where(
            part == member >> 1, 0 if slot == 0 else 2 if slot == images else 1, kind & 1
        )
        rows = pl.ds(pl.multiple_of(at * unit, unit), unit)
        for half in range(2):
            out_ref[slot * unit : (slot + 1) * unit, half * filters : (half + 1) * filters] = placed[
                2 * part + half, rows, :
            ]


def exchange(x, other):
    size = lax.axis_size("dp")
    return lax.ppermute(x, "dp", [(i, i ^ other) for i in range(size)])


def swap_cores(x):
    return lax.ppermute(x, "mp", [(0, 1), (1, 0)])


def f32(*shape):
    return jax.ShapeDtypeStruct(shape, jnp.float32)


ORDER = (1, 6, 2, 5, 4, 3, 7)
EARLY = (1, 6, 2, 5)
COST = 10**10
BATCHES = ((0, 1, 6), (2, 5, 4, 3), (7,))


def spread(messages):
    received = {0: messages[0]}
    for other in ORDER:
        received[other] = exchange(messages[other], other)
    return received


def local_cube(preact, weights, cotangent):
    extent, own_channels = preact.shape[2], preact.shape[3]
    pixels = preact.shape[1] * preact.shape[2]
    filters, taps, channels = weights.shape
    images = taps - 1
    lanes = own_channels // 4
    unit = channels // lax.axis_size("dp")
    depth = 2 * lanes * taps
    half = depth // 2

    small = pl.CostEstimate(flops=1, bytes_accessed=1, transcendentals=0)

    before = preact.reshape(pixels, own_channels)
    upstream = cotangent.reshape(pixels, filters)
    activity, *sent = pl.pallas_call(
        prepare_kernel,
        in_specs=[VMEM, VMEM],
        out_specs=[VMEM] * (1 + images),
        out_shape=[f32(pixels, own_channels)] + [f32(2, pixels, lanes)] * images,
        compiler_params=params(32),
        cost_estimate=small,
        name="prepare",
    )(before, upstream)
    messages = spread(sent)

    leaves, products = None, None
    known = ()
    for batch in BATCHES:
        last = len(known) + len(batch) == images
        size = len(batch)
        if known:
            arrived, leaves = lax.optimization_barrier(([messages[i] for i in batch], leaves))
            messages.update(zip(batch, arrived))
        operands = [messages[i] for i in batch] + [swap_cores(messages[i][0]) for i in batch]
        aliases = {}
        if known:
            aliases = {len(operands) + 1: 0}
            operands += [products, leaves]
        scratch = [
            pltpu.VMEM((size, 2 * lanes, 3 * pixels), jnp.bfloat16),
            pltpu.VMEM((size, 3 * pixels, taps * lanes), jnp.bfloat16),
        ]
        if last:
            scratch.append(pltpu.VMEM((images * images, lanes), jnp.float32))
        leaves, products = pl.pallas_call(
            functools.partial(leaf_kernel, extent, images, known, batch),
            in_specs=[VMEM] * len(operands),
            out_specs=[VMEM, VMEM],
            out_shape=[
                f32(images, depth, lanes),
                f32(-(-len(pairs(images)) // 8) * 8 if last else images * images, lanes),
            ],
            scratch_shapes=scratch,
            input_output_aliases=aliases,
            compiler_params=params(24),
            cost_estimate=small,
        name="leaf",
        )(*operands)
        known += batch
    gram = products
    for bit in range(3):
        gram = gram + from_partner(gram, "dp", bit)
    gram = gram + swap_cores(gram)

    piece = pl.pallas_call(
        far_kernel,
        in_specs=[VMEM, VMEM],
        out_specs=VMEM,
        out_shape=f32(half, lanes),
        compiler_params=params(24),
        cost_estimate=small,
        name="far",
    )(gram, leaves)
    far = exchange(piece, images)

    own, *own_sent = pl.pallas_call(
        functools.partial(own_kernel, unit),
        in_specs=[VMEM, VMEM],
        out_specs=[VMEM] * (1 + len(EARLY)),
        out_shape=[f32(half, lanes)] + [f32(units(other) * unit, lanes) for other in EARLY],
        compiler_params=params(24),
        cost_estimate=small,
        name="own",
    )(gram, leaves)
    own_messages = [exchange(message, other) for message, other in zip(own_sent, EARLY)]

    activity, piece = lax.optimization_barrier((activity, piece))
    output, kept, given = pl.pallas_call(
        functools.partial(image_kernel, extent),
        grid=(taps,),
        in_specs=[VMEM, VMEM, VMEM, pl.BlockSpec((1, filters, channels), lambda t: (t, 0, 0))],
        out_specs=[VMEM] * 3,
        out_shape=[f32(pixels, filters), f32(pixels, own_channels), f32(pixels, own_channels)],
        scratch_shapes=[
            pltpu.VMEM((pixels + 2 * extent, channels), jnp.bfloat16),
            pltpu.VMEM((pixels + 2 * extent, channels), jnp.bfloat16),
            pltpu.VMEM((3, pixels + 2 * extent, filters), jnp.bfloat16),
            pltpu.VMEM((3, pixels + 2 * extent, filters), jnp.bfloat16),
            pltpu.VMEM((3, pixels, filters), jnp.float32),
            pltpu.VMEM((pixels, channels), jnp.float32),
        ],
        compiler_params=params(44),
        cost_estimate=pl.CostEstimate(flops=COST, bytes_accessed=1, transcendentals=0),
        name="image",
    )(activity, swap_cores(activity), upstream, weights.transpose(1, 0, 2))
    input_grad = (kept + swap_cores(given)) * gelu_slope(before)

    far, own_messages = lax.optimization_barrier((far, own_messages))
    far_sent = pl.pallas_call(
        functools.partial(moments_kernel, unit),
        in_specs=[VMEM, VMEM],
        out_specs=[VMEM] * images,
        out_shape=[
            f32(8 + (1 if other in EARLY else 2) * units(other) * unit, lanes) for other in range(images)
        ],
        compiler_params=params(24),
        cost_estimate=small,
        name="moments",
    )(own, far)
    far_messages = spread(far_sent)
    moments = functools.reduce(jnp.add, [far_messages[i][0:8] for i in range(images)])
    moments = moments + swap_cores(moments)
    moments = moments + exchange(moments, images)
    weight_grad = pl.pallas_call(
        functools.partial(finish_kernel, unit, images),
        in_specs=[VMEM] * (1 + images + len(EARLY)),
        out_specs=VMEM,
        out_shape=f32(taps * unit, filters),
        scratch_shapes=[pltpu.VMEM((images, 3 * unit, lanes), jnp.float32)],
        compiler_params=params(24),
        cost_estimate=small,
        name="finish",
    )(moments, *[far_messages[i] for i in range(images)], *own_messages)
    return (
        output.reshape(cotangent.shape),
        input_grad.reshape(preact.shape),
        weight_grad.T,
    )


def local(preact, weights, cotangent):
    count, rows, extent, channels = preact.shape
    filters, taps = weights.shape[:2]
    fits = (
        count == 1
        and taps == 9
        and extent % 16 == 0
        and lax.axis_size("mp") == 2
        and lax.axis_size("dp") == 2 * (taps - 1)
        and channels == 4 * 128
        and filters == 2 * 128
    )
    if fits:
        return local_cube(preact, weights, cotangent)
    return local_any(preact, weights, cotangent)


def solution(mesh):
    in_specs = (P("dp", None, None, "mp"), P("mp", None, None), P("dp", None, None, "mp"))
    out_specs = (P("dp", None, None, "mp"), P("dp", None, None, "mp"), P("mp", "dp"))
    return jax.shard_map(local, mesh=mesh, in_specs=in_specs, out_specs=out_specs, check_vma=False)
```

```python
import functools

import jax
import jax.numpy as jnp
from jax import lax
from jax.experimental import pallas as pl
from jax.experimental.pallas import tpu as pltpu
from jax.sharding import PartitionSpec as P

highest = lax.Precision.HIGHEST
epsilon = 1e-06
MIB = 1 << 20


def from_partner(x, axis, apart):
    return lax.ppermute(x, axis, [(i, i ^ 1 << apart) for i in range(lax.axis_size(axis))])


def activate(values):
    return 0.5 * values * (1.0 + lax.erf(values * 0.7071067811865476))


def gelu_slope(values):
    return (
        0.5 * (1.0 + lax.erf(values * 0.7071067811865476))
        + values * jnp.exp(-0.5 * values * values) * 0.3989422804014327
    )


def pad_image(values):
    return jnp.pad(values, ((0, 0), (1, 1), (1, 1), (0, 0)))


def convolve_piece(activity, filters):
    extent = activity.shape[1]
    padded = pad_image(activity)
    summed = jnp.zeros(activity.shape[:3] + (filters.shape[0],), jnp.float32)
    for kernel_tap in range(9):
        row_shift, column_shift = divmod(kernel_tap, 3)
        window = padded[:, row_shift : row_shift + extent, column_shift : column_shift + extent, :]
        summed = summed + jnp.einsum(
            "nhwc,oc->nhwo", window, filters[:, kernel_tap, :], precision=highest
        )
    return summed


def weight_piece(activity, upstream):
    extent = activity.shape[1]
    padded = pad_image(activity)
    tap_grads = []
    for kernel_tap in range(9):
        row_shift, column_shift = divmod(kernel_tap, 3)
        window = padded[:, row_shift : row_shift + extent, column_shift : column_shift + extent, :]
        tap_grads.append(jnp.einsum("nhwo,nhwc->oc", upstream, window, precision=highest))
    return jnp.stack(tap_grads, 1)


def input_partial(upstream, filters):
    extent = upstream.shape[1]
    padded = pad_image(upstream)
    summed = jnp.zeros(upstream.shape[:3] + (filters.shape[2],), jnp.float32)
    for kernel_tap in range(9):
        row_shift, column_shift = divmod(kernel_tap, 3)
        window = padded[
            :,
            2 - row_shift : 2 - row_shift + extent,
            2 - column_shift : 2 - column_shift + extent,
            :,
        ]
        summed = summed + jnp.einsum(
            "nhwo,oc->nhwc", window, filters[:, kernel_tap, :], precision=highest
        )
    return summed


def adasum_halving(gradient):
    filter_count = gradient.shape[0]
    groups = lax.axis_size("dp")
    height = groups.bit_length() - 1
    data_index = lax.axis_index("dp")
    breadth = gradient.shape[1] * gradient.shape[2] // groups
    current = gradient.reshape(filter_count, groups, breadth)
    for section in range(height):
        parity = data_index >> section & 1
        paired = current.reshape(filter_count, current.shape[1] // 2, 2, breadth)
        kept_rows = lax.dynamic_slice_in_dim(paired, parity, 1, 2)[:, :, 0]
        sent_rows = lax.dynamic_slice_in_dim(paired, 1 - parity, 1, 2)[:, :, 0]
        partner = from_partner(sent_rows, "dp", section)
        lower = parity == 0
        leading = jnp.where(lower, kept_rows, partner)
        second = jnp.where(lower, partner, kept_rows)
        moments = jnp.stack(
            [jnp.sum(leading * second), jnp.sum(leading * leading), jnp.sum(second * second)]
        )
        for bit_level in range(section + 1):
            moments = moments + from_partner(moments, "dp", bit_level)
        moments = lax.psum(moments, "mp")
        cross = moments[0]
        lead_sq = moments[1]
        second_sq = moments[2]
        current = (1.0 - cross / (2.0 * (lead_sq + epsilon))) * leading + (
            1.0 - cross / (2.0 * (second_sq + epsilon))
        ) * second
    return current.reshape(filter_count, breadth)


def local_any(preact, weights, cotangent):
    activity = activate(preact)
    positions = preact.shape[0] * preact.shape[1] * preact.shape[2]
    output = convolve_piece(lax.all_gather(activity, "mp", axis=3, tiled=True), weights)
    gradient = weight_piece(lax.all_gather(activity, "mp", axis=3, tiled=True), cotangent)
    partial_sum = input_partial(cotangent, weights)
    input_grad = lax.psum_scatter(partial_sum, "mp", scatter_dimension=3, tiled=True) * gelu_slope(
        preact
    )
    weight_grad = adasum_halving(gradient / float(positions))
    return (output, input_grad, weight_grad)


VMEM = pl.BlockSpec(memory_space=pltpu.VMEM)


def params(limit):
    return pltpu.CompilerParams(vmem_limit_bytes=limit * MIB)


def split(values):
    high = values.astype(jnp.bfloat16)
    low = (values - high.astype(jnp.float32)).astype(jnp.bfloat16)
    return high, low


def dot(left, right, contract):
    return lax.dot_general(
        left, right, (contract, ((), ())), preferred_element_type=jnp.float32
    )


def dot3(left, right, contract):
    lh, ll = left
    rh, rl = right
    return dot(lh, rh, contract) + (dot(lh, rl, contract) + dot(ll, rh, contract))


def shifted(values, offset, extent):
    if offset == 0:
        return values
    rows = values.shape[0]
    column = lax.rem(lax.broadcasted_iota(jnp.int32, values.shape, 0), extent)
    if offset == 1:
        moved = jnp.concatenate([values[rows - 1 :], values[: rows - 1]], 0)
        return jnp.where(column >= 1, moved, 0.0)
    moved = jnp.concatenate([values[1:], values[:1]], 0)
    return jnp.where(column < extent - 1, moved, 0.0)


def aligned(index, size):
    return pl.ds(pl.multiple_of(index * size, size), size)


def place():
    index = lax.axis_index("dp")
    return index & 7, index >> 3, lax.axis_index("mp")


def prepare_kernel(preact_ref, up_ref, act_ref, *message_refs):
    act_ref[...] = activate(preact_ref[...])
    member = place()[0]
    channels = message_refs[0].shape[2]
    for other, message in enumerate(message_refs):
        target = member ^ other
        message[0] = act_ref[:, aligned(target >> 1, channels)]
        message[1] = up_ref[:, aligned(target & 1, channels)]


def image_kernel(extent, mine_ref, theirs_ref, up_ref, weight_ref,
                 out_ref, keep_ref, send_ref,
                 act_high, act_low, up_high, up_low, total, back):
    step = pl.program_id(0)
    pixels, channels = mine_ref.shape
    core = place()[2]

    @pl.when(step == 0)
    def _():
        for ref in (act_high, act_low):
            ref[...] = jnp.zeros_like(ref)
        for part, at in ((mine_ref, core), (theirs_ref, 1 - core)):
            high, low = split(part[...])
            act_high[extent : extent + pixels, aligned(at, channels)] = high
            act_low[extent : extent + pixels, aligned(at, channels)] = low
        for ref in (up_high, up_low):
            ref[...] = jnp.zeros_like(ref)
        for column in range(3):
            high, low = split(shifted(up_ref[...], column - 1, extent))
            up_high[column, extent : extent + pixels] = high
            up_low[column, extent : extent + pixels] = low
        total[...] = jnp.zeros_like(total)
        back[...] = jnp.zeros_like(back)

    row, column = step // 3, lax.rem(step, 3)
    weight = split(weight_ref[0])
    window = pl.ds(pl.multiple_of(row * extent, extent), pixels)
    total[column] += dot3((act_high[window, :], act_low[window, :]), weight, ((1,), (1,)))
    window = pl.ds(pl.multiple_of((2 - row) * extent, extent), pixels)
    back[...] += dot3((up_high[column, window], up_low[column, window]), weight, ((1,), (0,)))

    @pl.when(step == pl.num_programs(0) - 1)
    def _():
        out_ref[...] = (
            shifted(total[0], 1, extent) + total[1] + shifted(total[2], -1, extent)
        )
        keep_ref[...] = back[:, aligned(core, channels)]
        send_ref[...] = back[:, aligned(1 - core, channels)]


def pairs(count):
    return [(i, j) for i in range(count) for j in range(i, count)]


def leaf_kernel(extent, images, known, others, *refs):
    count = len(others)
    messages, swapped = refs[:count], refs[count : 2 * count]
    refs = refs[2 * count :]
    if known:
        products_in, _ = refs[:2]
        refs = refs[2:]
    leaf, products_ref, left, right = refs[:4]
    pixels, filters = messages[0].shape[1:]
    member, _, core = place()
    scale = 1.0 / pixels
    channels = filters
    depth = 2 * channels

    for at, other in enumerate(others):
        for part, where in ((messages[at][0], core), (swapped[at][...], 1 - core)):
            high, low = split(part.T)
            rows = aligned(where, channels)
            left[at, rows, 0:pixels] = high
            left[at, rows, pixels : 2 * pixels] = high
            left[at, rows, 2 * pixels : 3 * pixels] = low
        for column in range(3):
            moved = shifted(messages[at][1] * scale, column - 1, extent)
            gap = jnp.zeros((extent, filters), jnp.float32)
            for row in range(3):
                if row == 0:
                    placed = jnp.concatenate([moved[extent:], gap], 0)
                elif row == 2:
                    placed = jnp.concatenate([gap, moved[: pixels - extent]], 0)
                else:
                    placed = moved
                high, low = split(placed)
                tap = 3 * row + column
                lanes = slice(tap * filters, (tap + 1) * filters)
                right[at, 0:pixels, lanes] = high
                right[at, pixels : 2 * pixels, lanes] = low
                right[at, 2 * pixels : 3 * pixels, lanes] = high
        product = dot(left[at], right[at], ((1,), (0,)))
        image = member ^ other
        for tap in range(9):
            leaf[image, tap * depth : (tap + 1) * depth, :] = product[
                :, tap * filters : (tap + 1) * filters
            ]

    fresh = [(i, j) for at, i in enumerate(others) for j in list(known) + list(others[: at + 1])]
    held = list(known) + list(others)

    def add(chunk, sums):
        rows = pl.ds(pl.multiple_of(chunk * 8, 8), 8)
        blocks = {i: leaf[member ^ i, rows, :] for i in held}
        return tuple(s + blocks[i] * blocks[j] for s, (i, j) in zip(sums, fresh))

    zero = jnp.zeros((8, filters), jnp.float32)
    sums = lax.fori_loop(0, leaf.shape[1] // 8, add, tuple(zero for _ in fresh), unroll=4)
    table = products_ref if len(held) < images else refs[4]
    if known:
        table[...] = products_in[...]
    else:
        table[...] = jnp.zeros_like(table)
    for block, (i, j) in zip(sums, fresh):
        line = jnp.sum(block, 0, keepdims=True)
        table[i * images + j : i * images + j + 1, :] = line
        table[j * images + i : j * images + i + 1, :] = line
    if len(held) == images:
        products_ref[...] = jnp.zeros_like(products_ref)
        for at, (i, j) in enumerate(pairs(images)):
            products_ref[at : at + 1, :] = table[pl.ds((member ^ i) * images + (member ^ j), 1), :]


def factors(cross, lead_sq, second_sq):
    return (
        1.0 - cross / (2.0 * (lead_sq + epsilon)),
        1.0 - cross / (2.0 * (second_sq + epsilon)),
    )


def tree_factors(gram, images):
    inner = {pair: gram[at : at + 1, :] for at, pair in enumerate(pairs(images))}
    held = [1.0] * images
    count, width = images, 1
    while count > 1:
        scaled = []
        for node in range(0, count, 2):
            scaled += factors(
                inner[node, node + 1],
                jnp.maximum(inner[node, node], 0.0),
                jnp.maximum(inner[node + 1, node + 1], 0.0),
            )
        held = [value * scaled[at // width] for at, value in enumerate(held)]
        merged = {}
        for i, j in pairs(count // 2):
            terms = [
                scaled[2 * i + u] * scaled[2 * j + v] * inner[min(2 * i + u, 2 * j + v), max(2 * i + u, 2 * j + v)]
                for u in range(2)
                for v in range(2)
            ]
            merged[i, j] = (terms[0] + terms[1]) + (terms[2] + terms[3])
        inner, count, width = merged, count // 2, 2 * width
    return held


def combine(held, leaf_ref, start, out_ref):
    size = 64

    def some(chunk, carry):
        at = pl.multiple_of(start + chunk * size, size)
        total = held[0] * leaf_ref[0, pl.ds(at, size), :]
        for image in range(1, len(held)):
            total = total + held[image] * leaf_ref[image, pl.ds(at, size), :]
        out_ref[pl.ds(pl.multiple_of(chunk * size, size), size), :] = total
        return carry

    lax.fori_loop(0, out_ref.shape[0] // size, some, 0)


def combine_kernel(unit, gram_ref, leaf_ref, far_ref, own_ref, *message_refs):
    images = leaf_ref.shape[0]
    member, cube, _ = place()
    half = own_ref.shape[0]
    held = tree_factors(jnp.sum(gram_ref[...], 1, keepdims=True), images)
    combine(held, leaf_ref, (1 - cube) * half, far_ref)
    combine(held, leaf_ref, cube * half, own_ref)
    for other, message in zip(EARLY, message_refs):
        pack(member, own_ref, message, other, unit, 0)


def first_unit(target, part):
    low = 2 * part
    return jnp.where(low >= target, 2 * target, jnp.where(low + 1 >= target, 2 * target + 1, 2 * target + 2))


def units(other):
    return 3 if other < 2 else 2


def pack(member, source_ref, message, other, unit, start):
    first = first_unit(member ^ other, member >> 1)
    rows = units(other) * unit
    message[start : start + rows, :] = source_ref[pl.ds(pl.multiple_of(first * unit, unit), rows), :]


def moments_kernel(unit, own_ref, far_ref, *message_refs):
    member, cube, _ = place()
    lower = cube == 0
    own, far = own_ref[...], far_ref[...]
    cross = jnp.sum(own * far, 0, keepdims=True)
    own_sq = jnp.sum(own * own, 0, keepdims=True)
    far_sq = jnp.sum(far * far, 0, keepdims=True)
    lead_sq = jnp.where(lower, own_sq, far_sq)
    second_sq = jnp.where(lower, far_sq, own_sq)
    rest = jnp.zeros((5, own.shape[1]), jnp.float32)
    block = jnp.concatenate([cross, lead_sq, second_sq, rest], 0)
    for other, message in enumerate(message_refs):
        message[0:8, :] = block
        pack(member, far_ref, message, other, unit, 8)
        if other not in EARLY:
            pack(member, own_ref, message, other, unit, 8 + units(other) * unit)


def finish_kernel(unit, images, moments_ref, *refs):
    far, own = refs[:images], refs[images:-2]
    out_ref, placed = refs[-2:]
    member, cube, _ = place()
    lower = cube == 0
    moments = jnp.sum(moments_ref[...], 1, keepdims=True)
    lead, second = factors(moments[0:1], moments[1:2], moments[2:3])
    own_factor = jnp.where(lower, lead, second)
    far_factor = jnp.where(lower, second, lead)
    filters = placed.shape[2]
    for other in range(images):
        rows = units(other) * unit
        own_rows = own[EARLY.index(other)][...] if other in EARLY else far[other][8 + rows :, :]
        placed[member ^ other, 0:rows, :] = own_factor * own_rows + far_factor * far[other][8 : 8 + rows, :]
    for slot in range(images + 1):
        kind = (member + slot) & (images - 1)
        part = kind >> 1
        at = jnp.where(
            part == member >> 1, 0 if slot == 0 else 2 if slot == images else 1, kind & 1
        )
        rows = pl.ds(pl.multiple_of(at * unit, unit), unit)
        for half in range(2):
            out_ref[slot * unit : (slot + 1) * unit, half * filters : (half + 1) * filters] = placed[
                2 * part + half, rows, :
            ]


def exchange(x, other):
    size = lax.axis_size("dp")
    return lax.ppermute(x, "dp", [(i, i ^ other) for i in range(size)])


def swap_cores(x):
    return lax.ppermute(x, "mp", [(0, 1), (1, 0)])


def f32(*shape):
    return jax.ShapeDtypeStruct(shape, jnp.float32)


ORDER = (1, 6, 2, 5, 4, 3, 7)
EARLY = (1, 3, 5, 7)
LAST = (6, 1, 2, 5, 4, 3, 7)
COST = 10**10
BATCHES = ((0, 1, 6), (2, 5, 4, 3), (7,))


def spread(messages):
    received = {0: messages[0]}
    for other in ORDER:
        received[other] = exchange(messages[other], other)
    return received


def local_cube(preact, weights, cotangent):
    extent, own_channels = preact.shape[2], preact.shape[3]
    pixels = preact.shape[1] * preact.shape[2]
    filters, taps, channels = weights.shape
    images = taps - 1
    lanes = own_channels // 4
    unit = channels // lax.axis_size("dp")
    depth = 2 * lanes * taps
    half = depth // 2

    small = pl.CostEstimate(flops=1, bytes_accessed=1, transcendentals=0)

    before = preact.reshape(pixels, own_channels)
    upstream = cotangent.reshape(pixels, filters)
    activity, *sent = pl.pallas_call(
        prepare_kernel,
        in_specs=[VMEM] * 2,
        out_specs=[VMEM] * (1 + images),
        out_shape=[f32(pixels, own_channels)] + [f32(2, pixels, lanes)] * images,
        compiler_params=params(24),
        cost_estimate=small,
        name="prepare",
    )(before, upstream)
    messages = spread(sent)

    leaves, products = None, None
    known = ()
    for batch in BATCHES:
        last = len(known) + len(batch) == images
        size = len(batch)
        if known:
            arrived, leaves = lax.optimization_barrier(([messages[i] for i in batch], leaves))
            messages.update(zip(batch, arrived))
        operands = [messages[i] for i in batch] + [swap_cores(messages[i][0]) for i in batch]
        aliases = {}
        if known:
            aliases = {len(operands) + 1: 0}
            operands += [products, leaves]
        scratch = [
            pltpu.VMEM((size, 2 * lanes, 3 * pixels), jnp.bfloat16),
            pltpu.VMEM((size, 3 * pixels, taps * lanes), jnp.bfloat16),
        ]
        if last:
            scratch.append(pltpu.VMEM((images * images, lanes), jnp.float32))
        leaves, products = pl.pallas_call(
            functools.partial(leaf_kernel, extent, images, known, batch),
            in_specs=[VMEM] * len(operands),
            out_specs=[VMEM, VMEM],
            out_shape=[
                f32(images, depth, lanes),
                f32(-(-len(pairs(images)) // 8) * 8 if last else images * images, lanes),
            ],
            scratch_shapes=scratch,
            input_output_aliases=aliases,
            compiler_params=params(24),
            cost_estimate=small,
        name="leaf",
        )(*operands)
        known += batch
    gram = products
    for bit in range(3):
        gram = gram + from_partner(gram, "dp", bit)
    gram = gram + swap_cores(gram)

    theirs = swap_cores(activity)
    gram, theirs = lax.optimization_barrier((gram, theirs))
    piece, own, *own_sent = pl.pallas_call(
        functools.partial(combine_kernel, unit),
        in_specs=[VMEM, VMEM],
        out_specs=[VMEM] * (2 + len(EARLY)),
        out_shape=[f32(half, lanes)] * 2 + [f32(units(other) * unit, lanes) for other in EARLY],
        compiler_params=params(24),
        cost_estimate=small,
        name="combine",
    )(gram, leaves)
    far = exchange(piece, images)
    own_messages = [exchange(message, other) for message, other in zip(own_sent, EARLY)]

    activity, piece = lax.optimization_barrier((activity, piece))
    output, kept, given = pl.pallas_call(
        functools.partial(image_kernel, extent),
        grid=(taps,),
        in_specs=[VMEM, VMEM, VMEM, pl.BlockSpec((1, filters, channels), lambda t: (t, 0, 0))],
        out_specs=[VMEM] * 3,
        out_shape=[f32(pixels, filters), f32(pixels, own_channels), f32(pixels, own_channels)],
        scratch_shapes=[
            pltpu.VMEM((pixels + 2 * extent, channels), jnp.bfloat16),
            pltpu.VMEM((pixels + 2 * extent, channels), jnp.bfloat16),
            pltpu.VMEM((3, pixels + 2 * extent, filters), jnp.bfloat16),
            pltpu.VMEM((3, pixels + 2 * extent, filters), jnp.bfloat16),
            pltpu.VMEM((3, pixels, filters), jnp.float32),
            pltpu.VMEM((pixels, channels), jnp.float32),
        ],
        compiler_params=params(44),
        cost_estimate=pl.CostEstimate(flops=COST, bytes_accessed=1, transcendentals=0),
        name="image",
    )(activity, theirs, upstream, weights.transpose(1, 0, 2))
    input_grad = (kept + swap_cores(given)) * gelu_slope(before)

    far, own_messages, output = lax.optimization_barrier((far, own_messages, output))
    far_sent = pl.pallas_call(
        functools.partial(moments_kernel, unit),
        in_specs=[VMEM, VMEM],
        out_specs=[VMEM] * images,
        out_shape=[
            f32(8 + (1 if other in EARLY else 2) * units(other) * unit, lanes) for other in range(images)
        ],
        compiler_params=params(24),
        cost_estimate=small,
        name="moments",
    )(own, far)
    far_messages = {0: far_sent[0]}
    for other in LAST:
        far_messages[other] = exchange(far_sent[other], other)
    moments = far_sent[0][0:8]
    for other in LAST:
        moments, far_messages[other] = lax.optimization_barrier((moments, far_messages[other]))
        moments = moments + far_messages[other][0:8]
    moments = moments + swap_cores(moments)
    moments = moments + exchange(moments, images)
    moments, input_grad = lax.optimization_barrier((moments, input_grad))
    weight_grad = pl.pallas_call(
        functools.partial(finish_kernel, unit, images),
        in_specs=[VMEM] * (1 + images + len(EARLY)),
        out_specs=VMEM,
        out_shape=f32(taps * unit, filters),
        scratch_shapes=[pltpu.VMEM((images, 3 * unit, lanes), jnp.float32)],
        compiler_params=params(24),
        cost_estimate=small,
        name="finish",
    )(moments, *[far_messages[i] for i in range(images)], *own_messages)
    return (
        output.reshape(cotangent.shape),
        input_grad.reshape(preact.shape),
        weight_grad.T,
    )


def local(preact, weights, cotangent):
    count, rows, extent, channels = preact.shape
    filters, taps = weights.shape[:2]
    fits = (
        count == 1
        and taps == 9
        and extent % 16 == 0
        and lax.axis_size("mp") == 2
        and lax.axis_size("dp") == 2 * (taps - 1)
        and channels == 4 * 128
        and filters == 2 * 128
    )
    if fits:
        return local_cube(preact, weights, cotangent)
    return local_any(preact, weights, cotangent)


def solution(mesh):
    in_specs = (P("dp", None, None, "mp"), P("mp", None, None), P("dp", None, None, "mp"))
    out_specs = (P("dp", None, None, "mp"), P("dp", None, None, "mp"), P("mp", "dp"))
    return jax.shard_map(local, mesh=mesh, in_specs=in_specs, out_specs=out_specs, check_vma=False)
```

```python
import functools

import jax
import jax.numpy as jnp
from jax import lax
from jax.experimental import pallas as pl
from jax.experimental.pallas import tpu as pltpu
from jax.sharding import PartitionSpec as P

highest = lax.Precision.HIGHEST
epsilon = 1e-06
MIB = 1 << 20


def from_partner(x, axis, apart):
    return lax.ppermute(x, axis, [(i, i ^ 1 << apart) for i in range(lax.axis_size(axis))])


def activate(values):
    return 0.5 * values * (1.0 + lax.erf(values * 0.7071067811865476))


def gelu_slope(values):
    return (
        0.5 * (1.0 + lax.erf(values * 0.7071067811865476))
        + values * jnp.exp(-0.5 * values * values) * 0.3989422804014327
    )


def pad_image(values):
    return jnp.pad(values, ((0, 0), (1, 1), (1, 1), (0, 0)))


def convolve_piece(activity, filters):
    extent = activity.shape[1]
    padded = pad_image(activity)
    summed = jnp.zeros(activity.shape[:3] + (filters.shape[0],), jnp.float32)
    for kernel_tap in range(9):
        row_shift, column_shift = divmod(kernel_tap, 3)
        window = padded[:, row_shift : row_shift + extent, column_shift : column_shift + extent, :]
        summed = summed + jnp.einsum(
            "nhwc,oc->nhwo", window, filters[:, kernel_tap, :], precision=highest
        )
    return summed


def weight_piece(activity, upstream):
    extent = activity.shape[1]
    padded = pad_image(activity)
    tap_grads = []
    for kernel_tap in range(9):
        row_shift, column_shift = divmod(kernel_tap, 3)
        window = padded[:, row_shift : row_shift + extent, column_shift : column_shift + extent, :]
        tap_grads.append(jnp.einsum("nhwo,nhwc->oc", upstream, window, precision=highest))
    return jnp.stack(tap_grads, 1)


def input_partial(upstream, filters):
    extent = upstream.shape[1]
    padded = pad_image(upstream)
    summed = jnp.zeros(upstream.shape[:3] + (filters.shape[2],), jnp.float32)
    for kernel_tap in range(9):
        row_shift, column_shift = divmod(kernel_tap, 3)
        window = padded[
            :,
            2 - row_shift : 2 - row_shift + extent,
            2 - column_shift : 2 - column_shift + extent,
            :,
        ]
        summed = summed + jnp.einsum(
            "nhwo,oc->nhwc", window, filters[:, kernel_tap, :], precision=highest
        )
    return summed


def adasum_halving(gradient):
    filter_count = gradient.shape[0]
    groups = lax.axis_size("dp")
    height = groups.bit_length() - 1
    data_index = lax.axis_index("dp")
    breadth = gradient.shape[1] * gradient.shape[2] // groups
    current = gradient.reshape(filter_count, groups, breadth)
    for section in range(height):
        parity = data_index >> section & 1
        paired = current.reshape(filter_count, current.shape[1] // 2, 2, breadth)
        kept_rows = lax.dynamic_slice_in_dim(paired, parity, 1, 2)[:, :, 0]
        sent_rows = lax.dynamic_slice_in_dim(paired, 1 - parity, 1, 2)[:, :, 0]
        partner = from_partner(sent_rows, "dp", section)
        lower = parity == 0
        leading = jnp.where(lower, kept_rows, partner)
        second = jnp.where(lower, partner, kept_rows)
        moments = jnp.stack(
            [jnp.sum(leading * second), jnp.sum(leading * leading), jnp.sum(second * second)]
        )
        for bit_level in range(section + 1):
            moments = moments + from_partner(moments, "dp", bit_level)
        moments = lax.psum(moments, "mp")
        cross = moments[0]
        lead_sq = moments[1]
        second_sq = moments[2]
        current = (1.0 - cross / (2.0 * (lead_sq + epsilon))) * leading + (
            1.0 - cross / (2.0 * (second_sq + epsilon))
        ) * second
    return current.reshape(filter_count, breadth)


def local_any(preact, weights, cotangent):
    activity = activate(preact)
    positions = preact.shape[0] * preact.shape[1] * preact.shape[2]
    output = convolve_piece(lax.all_gather(activity, "mp", axis=3, tiled=True), weights)
    gradient = weight_piece(lax.all_gather(activity, "mp", axis=3, tiled=True), cotangent)
    partial_sum = input_partial(cotangent, weights)
    input_grad = lax.psum_scatter(partial_sum, "mp", scatter_dimension=3, tiled=True) * gelu_slope(
        preact
    )
    weight_grad = adasum_halving(gradient / float(positions))
    return (output, input_grad, weight_grad)


VMEM = pl.BlockSpec(memory_space=pltpu.VMEM)


def params(limit):
    return pltpu.CompilerParams(vmem_limit_bytes=limit * MIB)


def split(values):
    high = values.astype(jnp.bfloat16)
    low = (values - high.astype(jnp.float32)).astype(jnp.bfloat16)
    return high, low


def dot(left, right, contract):
    return lax.dot_general(
        left, right, (contract, ((), ())), preferred_element_type=jnp.float32
    )


def dot3(left, right, contract):
    lh, ll = left
    rh, rl = right
    return dot(lh, rh, contract) + (dot(lh, rl, contract) + dot(ll, rh, contract))


def shifted(values, offset, extent):
    if offset == 0:
        return values
    rows = values.shape[0]
    column = lax.rem(lax.broadcasted_iota(jnp.int32, values.shape, 0), extent)
    if offset == 1:
        moved = jnp.concatenate([values[rows - 1 :], values[: rows - 1]], 0)
        return jnp.where(column >= 1, moved, 0.0)
    moved = jnp.concatenate([values[1:], values[:1]], 0)
    return jnp.where(column < extent - 1, moved, 0.0)


def aligned(index, size):
    return pl.ds(pl.multiple_of(index * size, size), size)


def place():
    index = lax.axis_index("dp")
    return index & 7, index >> 3, lax.axis_index("mp")


def prepare_kernel(preact_ref, up_ref, act_ref, *message_refs):
    act_ref[...] = activate(preact_ref[...])
    member = place()[0]
    channels = message_refs[0].shape[2]
    for other, message in enumerate(message_refs):
        target = member ^ other
        message[0] = act_ref[:, aligned(target >> 1, channels)]
        message[1] = up_ref[:, aligned(target & 1, channels)]


def image_kernel(extent, mine_ref, theirs_ref, up_ref, weight_ref,
                 out_ref, keep_ref, send_ref,
                 act_high, act_low, up_high, up_low, total, back):
    step = pl.program_id(0)
    pixels, channels = mine_ref.shape
    core = place()[2]

    @pl.when(step == 0)
    def _():
        for ref in (act_high, act_low):
            ref[...] = jnp.zeros_like(ref)
        for part, at in ((mine_ref, core), (theirs_ref, 1 - core)):
            high, low = split(part[...])
            act_high[extent : extent + pixels, aligned(at, channels)] = high
            act_low[extent : extent + pixels, aligned(at, channels)] = low
        for ref in (up_high, up_low):
            ref[...] = jnp.zeros_like(ref)
        for column in range(3):
            high, low = split(shifted(up_ref[...], column - 1, extent))
            up_high[column, extent : extent + pixels] = high
            up_low[column, extent : extent + pixels] = low
        total[...] = jnp.zeros_like(total)
        back[...] = jnp.zeros_like(back)

    row, column = step // 3, lax.rem(step, 3)
    weight = split(weight_ref[0])
    window = pl.ds(pl.multiple_of(row * extent, extent), pixels)
    total[column] += dot3((act_high[window, :], act_low[window, :]), weight, ((1,), (1,)))
    window = pl.ds(pl.multiple_of((2 - row) * extent, extent), pixels)
    back[...] += dot3((up_high[column, window], up_low[column, window]), weight, ((1,), (0,)))

    @pl.when(step == pl.num_programs(0) - 1)
    def _():
        out_ref[...] = (
            shifted(total[0], 1, extent) + total[1] + shifted(total[2], -1, extent)
        )
        keep_ref[...] = back[:, aligned(core, channels)]
        send_ref[...] = back[:, aligned(1 - core, channels)]


def pairs(count):
    return [(i, j) for i in range(count) for j in range(i, count)]


def leaf_kernel(extent, images, known, others, *refs):
    count = len(others)
    messages, swapped = refs[:count], refs[count : 2 * count]
    refs = refs[2 * count :]
    if known:
        products_in, _ = refs[:2]
        refs = refs[2:]
    leaf, products_ref, left, right = refs[:4]
    pixels, filters = messages[0].shape[1:]
    member, _, core = place()
    scale = 1.0 / pixels
    channels = filters
    depth = 2 * channels

    for at, other in enumerate(others):
        for part, where in ((messages[at][0], core), (swapped[at][...], 1 - core)):
            high, low = split(part.T)
            rows = aligned(where, channels)
            left[at, rows, 0:pixels] = high
            left[at, rows, pixels : 2 * pixels] = high
            left[at, rows, 2 * pixels : 3 * pixels] = low
        for column in range(3):
            moved = shifted(messages[at][1] * scale, column - 1, extent)
            gap = jnp.zeros((extent, filters), jnp.float32)
            for row in range(3):
                if row == 0:
                    placed = jnp.concatenate([moved[extent:], gap], 0)
                elif row == 2:
                    placed = jnp.concatenate([gap, moved[: pixels - extent]], 0)
                else:
                    placed = moved
                high, low = split(placed)
                tap = 3 * row + column
                lanes = slice(tap * filters, (tap + 1) * filters)
                right[at, 0:pixels, lanes] = high
                right[at, pixels : 2 * pixels, lanes] = low
                right[at, 2 * pixels : 3 * pixels, lanes] = high
        product = dot(left[at], right[at], ((1,), (0,)))
        image = member ^ other
        for tap in range(9):
            leaf[image, tap * depth : (tap + 1) * depth, :] = product[
                :, tap * filters : (tap + 1) * filters
            ]

    fresh = [(i, j) for at, i in enumerate(others) for j in list(known) + list(others[: at + 1])]
    held = list(known) + list(others)

    def add(chunk, sums):
        rows = pl.ds(pl.multiple_of(chunk * 8, 8), 8)
        blocks = {i: leaf[member ^ i, rows, :] for i in held}
        return tuple(s + blocks[i] * blocks[j] for s, (i, j) in zip(sums, fresh))

    zero = jnp.zeros((8, filters), jnp.float32)
    sums = lax.fori_loop(0, leaf.shape[1] // 8, add, tuple(zero for _ in fresh), unroll=4)
    table = products_ref if len(held) < images else refs[4]
    if known:
        table[...] = products_in[...]
    else:
        table[...] = jnp.zeros_like(table)
    for block, (i, j) in zip(sums, fresh):
        line = jnp.sum(block, 0, keepdims=True)
        table[i * images + j : i * images + j + 1, :] = line
        table[j * images + i : j * images + i + 1, :] = line
    if len(held) == images:
        products_ref[...] = jnp.zeros_like(products_ref)
        for at, (i, j) in enumerate(pairs(images)):
            products_ref[at : at + 1, :] = table[pl.ds((member ^ i) * images + (member ^ j), 1), :]


def factors(cross, lead_sq, second_sq):
    return (
        1.0 - cross / (2.0 * (lead_sq + epsilon)),
        1.0 - cross / (2.0 * (second_sq + epsilon)),
    )


def tree_factors(gram, images):
    inner = {pair: gram[at : at + 1, :] for at, pair in enumerate(pairs(images))}
    held = [1.0] * images
    count, width = images, 1
    while count > 1:
        scaled = []
        for node in range(0, count, 2):
            scaled += factors(
                inner[node, node + 1],
                jnp.maximum(inner[node, node], 0.0),
                jnp.maximum(inner[node + 1, node + 1], 0.0),
            )
        held = [value * scaled[at // width] for at, value in enumerate(held)]
        merged = {}
        for i, j in pairs(count // 2):
            terms = [
                scaled[2 * i + u] * scaled[2 * j + v] * inner[min(2 * i + u, 2 * j + v), max(2 * i + u, 2 * j + v)]
                for u in range(2)
                for v in range(2)
            ]
            merged[i, j] = (terms[0] + terms[1]) + (terms[2] + terms[3])
        inner, count, width = merged, count // 2, 2 * width
    return held


def combine(held, leaf_ref, start, out_ref):
    size = 64

    def some(chunk, carry):
        at = pl.multiple_of(start + chunk * size, size)
        total = held[0] * leaf_ref[0, pl.ds(at, size), :]
        for image in range(1, len(held)):
            total = total + held[image] * leaf_ref[image, pl.ds(at, size), :]
        out_ref[pl.ds(pl.multiple_of(chunk * size, size), size), :] = total
        return carry

    lax.fori_loop(0, out_ref.shape[0] // size, some, 0)


def combine_kernel(unit, gram_ref, leaf_ref, far_ref, own_ref, *message_refs):
    images = leaf_ref.shape[0]
    member, cube, _ = place()
    half = own_ref.shape[0]
    held = tree_factors(jnp.sum(gram_ref[...], 1, keepdims=True), images)
    combine(held, leaf_ref, (1 - cube) * half, far_ref)
    combine(held, leaf_ref, cube * half, own_ref)
    for other, message in zip(EARLY, message_refs):
        pack(member, own_ref, message, other, unit, 0)


def first_unit(target, part):
    low = 2 * part
    return jnp.where(low >= target, 2 * target, jnp.where(low + 1 >= target, 2 * target + 1, 2 * target + 2))


def units(other):
    return 3 if other < 2 else 2


def pack(member, source_ref, message, other, unit, start):
    first = first_unit(member ^ other, member >> 1)
    rows = units(other) * unit
    message[start : start + rows, :] = source_ref[pl.ds(pl.multiple_of(first * unit, unit), rows), :]


def moments_kernel(unit, own_ref, far_ref, *message_refs):
    member, cube, _ = place()
    lower = cube == 0
    own, far = own_ref[...], far_ref[...]
    cross = jnp.sum(own * far, 0, keepdims=True)
    own_sq = jnp.sum(own * own, 0, keepdims=True)
    far_sq = jnp.sum(far * far, 0, keepdims=True)
    lead_sq = jnp.where(lower, own_sq, far_sq)
    second_sq = jnp.where(lower, far_sq, own_sq)
    rest = jnp.zeros((5, own.shape[1]), jnp.float32)
    block = jnp.concatenate([cross, lead_sq, second_sq, rest], 0)
    for other, message in enumerate(message_refs):
        message[0:8, :] = block
        pack(member, far_ref, message, other, unit, 8)
        if other not in EARLY:
            pack(member, own_ref, message, other, unit, 8 + units(other) * unit)


def finish_kernel(unit, images, moments_ref, *refs):
    far, own = refs[:images], refs[images:-2]
    out_ref, placed = refs[-2:]
    member, cube, _ = place()
    lower = cube == 0
    moments = jnp.sum(moments_ref[...], 1, keepdims=True)
    lead, second = factors(moments[0:1], moments[1:2], moments[2:3])
    own_factor = jnp.where(lower, lead, second)
    far_factor = jnp.where(lower, second, lead)
    filters = placed.shape[2]
    for other in range(images):
        rows = units(other) * unit
        own_rows = own[EARLY.index(other)][...] if other in EARLY else far[other][8 + rows :, :]
        placed[member ^ other, 0:rows, :] = own_factor * own_rows + far_factor * far[other][8 : 8 + rows, :]
    for slot in range(images + 1):
        kind = (member + slot) & (images - 1)
        part = kind >> 1
        at = jnp.where(
            part == member >> 1, 0 if slot == 0 else 2 if slot == images else 1, kind & 1
        )
        rows = pl.ds(pl.multiple_of(at * unit, unit), unit)
        for half in range(2):
            out_ref[slot * unit : (slot + 1) * unit, half * filters : (half + 1) * filters] = placed[
                2 * part + half, rows, :
            ]


def exchange(x, other):
    size = lax.axis_size("dp")
    return lax.ppermute(x, "dp", [(i, i ^ other) for i in range(size)])


def swap_cores(x):
    return lax.ppermute(x, "mp", [(0, 1), (1, 0)])


def f32(*shape):
    return jax.ShapeDtypeStruct(shape, jnp.float32)


ORDER = (1, 6, 2, 5, 3, 4, 7)
EARLY = (1, 3, 5, 7)
LAST = (6, 1, 2, 5, 4, 3, 7)
COST = 10**10
BATCHES = ((0, 1, 6), (2, 5), (3, 4), (7,))


def spread(messages):
    received = {0: messages[0]}
    for other in ORDER:
        received[other] = exchange(messages[other], other)
    return received


def local_cube(preact, weights, cotangent):
    extent, own_channels = preact.shape[2], preact.shape[3]
    pixels = preact.shape[1] * preact.shape[2]
    filters, taps, channels = weights.shape
    images = taps - 1
    lanes = own_channels // 4
    unit = channels // lax.axis_size("dp")
    depth = 2 * lanes * taps
    half = depth // 2

    small = pl.CostEstimate(flops=1, bytes_accessed=1, transcendentals=0)

    before = preact.reshape(pixels, own_channels)
    upstream = cotangent.reshape(pixels, filters)
    activity, *sent = pl.pallas_call(
        prepare_kernel,
        in_specs=[VMEM] * 2,
        out_specs=[VMEM] * (1 + images),
        out_shape=[f32(pixels, own_channels)] + [f32(2, pixels, lanes)] * images,
        compiler_params=params(24),
        cost_estimate=small,
        name="prepare",
    )(before, upstream)
    messages = spread(sent)

    leaves, products = None, None
    known = ()
    for batch in BATCHES:
        last = len(known) + len(batch) == images
        size = len(batch)
        if known:
            arrived, leaves = lax.optimization_barrier(([messages[i] for i in batch], leaves))
            messages.update(zip(batch, arrived))
        operands = [messages[i] for i in batch] + [swap_cores(messages[i][0]) for i in batch]
        aliases = {}
        if known:
            aliases = {len(operands) + 1: 0}
            operands += [products, leaves]
        scratch = [
            pltpu.VMEM((size, 2 * lanes, 3 * pixels), jnp.bfloat16),
            pltpu.VMEM((size, 3 * pixels, taps * lanes), jnp.bfloat16),
        ]
        if last:
            scratch.append(pltpu.VMEM((images * images, lanes), jnp.float32))
        leaves, products = pl.pallas_call(
            functools.partial(leaf_kernel, extent, images, known, batch),
            in_specs=[VMEM] * len(operands),
            out_specs=[VMEM, VMEM],
            out_shape=[
                f32(images, depth, lanes),
                f32(-(-len(pairs(images)) // 8) * 8 if last else images * images, lanes),
            ],
            scratch_shapes=scratch,
            input_output_aliases=aliases,
            compiler_params=params(24),
            cost_estimate=small,
        name="leaf",
        )(*operands)
        known += batch
    gram = products
    gram = gram + exchange(gram, 1) + exchange(gram, 2) + exchange(gram, 3)
    gram = gram + exchange(gram, 4)
    gram = gram + swap_cores(gram)

    theirs = swap_cores(activity)
    gram, theirs = lax.optimization_barrier((gram, theirs))
    piece, own, *own_sent = pl.pallas_call(
        functools.partial(combine_kernel, unit),
        in_specs=[VMEM, VMEM],
        out_specs=[VMEM] * (2 + len(EARLY)),
        out_shape=[f32(half, lanes)] * 2 + [f32(units(other) * unit, lanes) for other in EARLY],
        compiler_params=params(24),
        cost_estimate=small,
        name="combine",
    )(gram, leaves)
    far = exchange(piece, images)
    own_messages = [exchange(message, other) for message, other in zip(own_sent, EARLY)]

    activity, piece = lax.optimization_barrier((activity, piece))
    output, kept, given = pl.pallas_call(
        functools.partial(image_kernel, extent),
        grid=(taps,),
        in_specs=[VMEM, VMEM, VMEM, pl.BlockSpec((1, filters, channels), lambda t: (t, 0, 0))],
        out_specs=[VMEM] * 3,
        out_shape=[f32(pixels, filters), f32(pixels, own_channels), f32(pixels, own_channels)],
        scratch_shapes=[
            pltpu.VMEM((pixels + 2 * extent, channels), jnp.bfloat16),
            pltpu.VMEM((pixels + 2 * extent, channels), jnp.bfloat16),
            pltpu.VMEM((3, pixels + 2 * extent, filters), jnp.bfloat16),
            pltpu.VMEM((3, pixels + 2 * extent, filters), jnp.bfloat16),
            pltpu.VMEM((3, pixels, filters), jnp.float32),
            pltpu.VMEM((pixels, channels), jnp.float32),
        ],
        compiler_params=params(44),
        cost_estimate=pl.CostEstimate(flops=COST, bytes_accessed=1, transcendentals=0),
        name="image",
    )(activity, theirs, upstream, weights.transpose(1, 0, 2))
    input_grad = (kept + swap_cores(given)) * gelu_slope(before)

    far, own_messages, output = lax.optimization_barrier((far, own_messages, output))
    far_sent = pl.pallas_call(
        functools.partial(moments_kernel, unit),
        in_specs=[VMEM, VMEM],
        out_specs=[VMEM] * images,
        out_shape=[
            f32(8 + (1 if other in EARLY else 2) * units(other) * unit, lanes) for other in range(images)
        ],
        compiler_params=params(24),
        cost_estimate=small,
        name="moments",
    )(own, far)
    far_messages = {0: far_sent[0]}
    for other in LAST:
        far_messages[other] = exchange(far_sent[other], other)
    moments = far_sent[0][0:8]
    for other in LAST:
        moments, far_messages[other] = lax.optimization_barrier((moments, far_messages[other]))
        moments = moments + far_messages[other][0:8]
    moments = moments + swap_cores(moments)
    moments = moments + exchange(moments, images)
    moments, input_grad = lax.optimization_barrier((moments, input_grad))
    weight_grad = pl.pallas_call(
        functools.partial(finish_kernel, unit, images),
        in_specs=[VMEM] * (1 + images + len(EARLY)),
        out_specs=VMEM,
        out_shape=f32(taps * unit, filters),
        scratch_shapes=[pltpu.VMEM((images, 3 * unit, lanes), jnp.float32)],
        compiler_params=params(24),
        cost_estimate=small,
        name="finish",
    )(moments, *[far_messages[i] for i in range(images)], *own_messages)
    return (
        output.reshape(cotangent.shape),
        input_grad.reshape(preact.shape),
        weight_grad.T,
    )


def local(preact, weights, cotangent):
    count, rows, extent, channels = preact.shape
    filters, taps = weights.shape[:2]
    fits = (
        count == 1
        and taps == 9
        and extent % 16 == 0
        and lax.axis_size("mp") == 2
        and lax.axis_size("dp") == 2 * (taps - 1)
        and channels == 4 * 128
        and filters == 2 * 128
    )
    if fits:
        return local_cube(preact, weights, cotangent)
    return local_any(preact, weights, cotangent)


def solution(mesh):
    in_specs = (P("dp", None, None, "mp"), P("mp", None, None), P("dp", None, None, "mp"))
    out_specs = (P("dp", None, None, "mp"), P("dp", None, None, "mp"), P("mp", "dp"))
    return jax.shard_map(local, mesh=mesh, in_specs=in_specs, out_specs=out_specs, check_vma=False)
```

```python
import functools

import jax
import jax.numpy as jnp
from jax import lax
from jax.experimental import pallas as pl
from jax.experimental.pallas import tpu as pltpu
from jax.sharding import PartitionSpec as P

highest = lax.Precision.HIGHEST
epsilon = 1e-06
MIB = 1 << 20


def from_partner(x, axis, apart):
    return lax.ppermute(x, axis, [(i, i ^ 1 << apart) for i in range(lax.axis_size(axis))])


def activate(values):
    return 0.5 * values * (1.0 + lax.erf(values * 0.7071067811865476))


def gelu_slope(values):
    return (
        0.5 * (1.0 + lax.erf(values * 0.7071067811865476))
        + values * jnp.exp(-0.5 * values * values) * 0.3989422804014327
    )


def pad_image(values):
    return jnp.pad(values, ((0, 0), (1, 1), (1, 1), (0, 0)))


def convolve_piece(activity, filters):
    extent = activity.shape[1]
    padded = pad_image(activity)
    summed = jnp.zeros(activity.shape[:3] + (filters.shape[0],), jnp.float32)
    for kernel_tap in range(9):
        row_shift, column_shift = divmod(kernel_tap, 3)
        window = padded[:, row_shift : row_shift + extent, column_shift : column_shift + extent, :]
        summed = summed + jnp.einsum(
            "nhwc,oc->nhwo", window, filters[:, kernel_tap, :], precision=highest
        )
    return summed


def weight_piece(activity, upstream):
    extent = activity.shape[1]
    padded = pad_image(activity)
    tap_grads = []
    for kernel_tap in range(9):
        row_shift, column_shift = divmod(kernel_tap, 3)
        window = padded[:, row_shift : row_shift + extent, column_shift : column_shift + extent, :]
        tap_grads.append(jnp.einsum("nhwo,nhwc->oc", upstream, window, precision=highest))
    return jnp.stack(tap_grads, 1)


def input_partial(upstream, filters):
    extent = upstream.shape[1]
    padded = pad_image(upstream)
    summed = jnp.zeros(upstream.shape[:3] + (filters.shape[2],), jnp.float32)
    for kernel_tap in range(9):
        row_shift, column_shift = divmod(kernel_tap, 3)
        window = padded[
            :,
            2 - row_shift : 2 - row_shift + extent,
            2 - column_shift : 2 - column_shift + extent,
            :,
        ]
        summed = summed + jnp.einsum(
            "nhwo,oc->nhwc", window, filters[:, kernel_tap, :], precision=highest
        )
    return summed


def adasum_halving(gradient):
    filter_count = gradient.shape[0]
    groups = lax.axis_size("dp")
    height = groups.bit_length() - 1
    data_index = lax.axis_index("dp")
    breadth = gradient.shape[1] * gradient.shape[2] // groups
    current = gradient.reshape(filter_count, groups, breadth)
    for section in range(height):
        parity = data_index >> section & 1
        paired = current.reshape(filter_count, current.shape[1] // 2, 2, breadth)
        kept_rows = lax.dynamic_slice_in_dim(paired, parity, 1, 2)[:, :, 0]
        sent_rows = lax.dynamic_slice_in_dim(paired, 1 - parity, 1, 2)[:, :, 0]
        partner = from_partner(sent_rows, "dp", section)
        lower = parity == 0
        leading = jnp.where(lower, kept_rows, partner)
        second = jnp.where(lower, partner, kept_rows)
        moments = jnp.stack(
            [jnp.sum(leading * second), jnp.sum(leading * leading), jnp.sum(second * second)]
        )
        for bit_level in range(section + 1):
            moments = moments + from_partner(moments, "dp", bit_level)
        moments = lax.psum(moments, "mp")
        cross = moments[0]
        lead_sq = moments[1]
        second_sq = moments[2]
        current = (1.0 - cross / (2.0 * (lead_sq + epsilon))) * leading + (
            1.0 - cross / (2.0 * (second_sq + epsilon))
        ) * second
    return current.reshape(filter_count, breadth)


def local_any(preact, weights, cotangent):
    activity = activate(preact)
    positions = preact.shape[0] * preact.shape[1] * preact.shape[2]
    output = convolve_piece(lax.all_gather(activity, "mp", axis=3, tiled=True), weights)
    gradient = weight_piece(lax.all_gather(activity, "mp", axis=3, tiled=True), cotangent)
    partial_sum = input_partial(cotangent, weights)
    input_grad = lax.psum_scatter(partial_sum, "mp", scatter_dimension=3, tiled=True) * gelu_slope(
        preact
    )
    weight_grad = adasum_halving(gradient / float(positions))
    return (output, input_grad, weight_grad)


VMEM = pl.BlockSpec(memory_space=pltpu.VMEM)


def params(limit):
    return pltpu.CompilerParams(vmem_limit_bytes=limit * MIB)


def split(values):
    high = values.astype(jnp.bfloat16)
    low = (values - high.astype(jnp.float32)).astype(jnp.bfloat16)
    return high, low


def dot(left, right, contract):
    return lax.dot_general(
        left, right, (contract, ((), ())), preferred_element_type=jnp.float32
    )


def dot3(left, right, contract):
    lh, ll = left
    rh, rl = right
    return dot(lh, rh, contract) + (dot(lh, rl, contract) + dot(ll, rh, contract))


def shifted(values, offset, extent):
    if offset == 0:
        return values
    rows = values.shape[0]
    column = lax.rem(lax.broadcasted_iota(jnp.int32, values.shape, 0), extent)
    if offset == 1:
        moved = jnp.concatenate([values[rows - 1 :], values[: rows - 1]], 0)
        return jnp.where(column >= 1, moved, 0.0)
    moved = jnp.concatenate([values[1:], values[:1]], 0)
    return jnp.where(column < extent - 1, moved, 0.0)


def aligned(index, size):
    return pl.ds(pl.multiple_of(index * size, size), size)


def place():
    index = lax.axis_index("dp")
    return index & 7, index >> 3, lax.axis_index("mp")


def prepare_kernel(preact_ref, up_ref, act_ref, *message_refs):
    act_ref[...] = activate(preact_ref[...])
    member = place()[0]
    channels = message_refs[0].shape[2]
    for other, message in enumerate(message_refs):
        target = member ^ other
        message[0] = act_ref[:, aligned(target >> 1, channels)]
        message[1] = up_ref[:, aligned(target & 1, channels)]


def image_kernel(extent, mine_ref, theirs_ref, up_ref, weight_ref,
                 out_ref, keep_ref, send_ref,
                 act_high, act_low, up_high, up_low, total, back):
    step = pl.program_id(0)
    pixels, channels = mine_ref.shape
    core = place()[2]

    @pl.when(step == 0)
    def _():
        for ref in (act_high, act_low):
            ref[...] = jnp.zeros_like(ref)
        for part, at in ((mine_ref, core), (theirs_ref, 1 - core)):
            high, low = split(part[...])
            act_high[extent : extent + pixels, aligned(at, channels)] = high
            act_low[extent : extent + pixels, aligned(at, channels)] = low
        for ref in (up_high, up_low):
            ref[...] = jnp.zeros_like(ref)
        for column in range(3):
            high, low = split(shifted(up_ref[...], column - 1, extent))
            up_high[column, extent : extent + pixels] = high
            up_low[column, extent : extent + pixels] = low
        total[...] = jnp.zeros_like(total)
        back[...] = jnp.zeros_like(back)

    row, column = step // 3, lax.rem(step, 3)
    weight = split(weight_ref[0])
    window = pl.ds(pl.multiple_of(row * extent, extent), pixels)
    total[column] += dot3((act_high[window, :], act_low[window, :]), weight, ((1,), (1,)))
    window = pl.ds(pl.multiple_of((2 - row) * extent, extent), pixels)
    back[...] += dot3((up_high[column, window], up_low[column, window]), weight, ((1,), (0,)))

    @pl.when(step == pl.num_programs(0) - 1)
    def _():
        out_ref[...] = (
            shifted(total[0], 1, extent) + total[1] + shifted(total[2], -1, extent)
        )
        keep_ref[...] = back[:, aligned(core, channels)]
        send_ref[...] = back[:, aligned(1 - core, channels)]


def pairs(count):
    return [(i, j) for i in range(count) for j in range(i, count)]


def leaf_kernel(extent, images, known, others, *refs):
    count = len(others)
    messages, swapped = refs[:count], refs[count : 2 * count]
    refs = refs[2 * count :]
    if known:
        products_in, _ = refs[:2]
        refs = refs[2:]
    leaf, products_ref, left, right = refs[:4]
    pixels, filters = messages[0].shape[1:]
    member, _, core = place()
    scale = 1.0 / pixels
    channels = filters
    depth = 2 * channels

    for at, other in enumerate(others):
        for part, where in ((messages[at][0], core), (swapped[at][...], 1 - core)):
            high, low = split(part.T)
            rows = aligned(where, channels)
            left[at, rows, 0:pixels] = high
            left[at, rows, pixels : 2 * pixels] = high
            left[at, rows, 2 * pixels : 3 * pixels] = low
        for column in range(3):
            moved = shifted(messages[at][1] * scale, column - 1, extent)
            gap = jnp.zeros((extent, filters), jnp.float32)
            for row in range(3):
                if row == 0:
                    placed = jnp.concatenate([moved[extent:], gap], 0)
                elif row == 2:
                    placed = jnp.concatenate([gap, moved[: pixels - extent]], 0)
                else:
                    placed = moved
                high, low = split(placed)
                tap = 3 * row + column
                lanes = slice(tap * filters, (tap + 1) * filters)
                right[at, 0:pixels, lanes] = high
                right[at, pixels : 2 * pixels, lanes] = low
                right[at, 2 * pixels : 3 * pixels, lanes] = high
        product = dot(left[at], right[at], ((1,), (0,)))
        image = member ^ other
        for tap in range(9):
            leaf[image, tap * depth : (tap + 1) * depth, :] = product[
                :, tap * filters : (tap + 1) * filters
            ]

    fresh = [(i, j) for at, i in enumerate(others) for j in list(known) + list(others[: at + 1])]
    held = list(known) + list(others)

    def add(chunk, sums):
        rows = pl.ds(pl.multiple_of(chunk * 8, 8), 8)
        blocks = {i: leaf[member ^ i, rows, :] for i in held}
        return tuple(s + blocks[i] * blocks[j] for s, (i, j) in zip(sums, fresh))

    zero = jnp.zeros((8, filters), jnp.float32)
    sums = lax.fori_loop(0, leaf.shape[1] // 8, add, tuple(zero for _ in fresh), unroll=4)
    table = products_ref if len(held) < images else refs[4]
    if known:
        table[...] = products_in[...]
    else:
        table[...] = jnp.zeros_like(table)
    for block, (i, j) in zip(sums, fresh):
        line = jnp.sum(block, 0, keepdims=True)
        table[i * images + j : i * images + j + 1, :] = line
        table[j * images + i : j * images + i + 1, :] = line
    if len(held) == images:
        products_ref[...] = jnp.zeros_like(products_ref)
        for at, (i, j) in enumerate(pairs(images)):
            products_ref[at : at + 1, :] = table[pl.ds((member ^ i) * images + (member ^ j), 1), :]


def factors(cross, lead_sq, second_sq):
    return (
        1.0 - cross / (2.0 * (lead_sq + epsilon)),
        1.0 - cross / (2.0 * (second_sq + epsilon)),
    )


def tree_factors(gram, images):
    inner = {pair: gram[at : at + 1, :] for at, pair in enumerate(pairs(images))}
    held = [1.0] * images
    count, width = images, 1
    while count > 1:
        scaled = []
        for node in range(0, count, 2):
            scaled += factors(
                inner[node, node + 1],
                jnp.maximum(inner[node, node], 0.0),
                jnp.maximum(inner[node + 1, node + 1], 0.0),
            )
        held = [value * scaled[at // width] for at, value in enumerate(held)]
        merged = {}
        for i, j in pairs(count // 2):
            terms = [
                scaled[2 * i + u] * scaled[2 * j + v] * inner[min(2 * i + u, 2 * j + v), max(2 * i + u, 2 * j + v)]
                for u in range(2)
                for v in range(2)
            ]
            merged[i, j] = (terms[0] + terms[1]) + (terms[2] + terms[3])
        inner, count, width = merged, count // 2, 2 * width
    return held


def combine(held, leaf_ref, start, out_ref):
    size = 64

    def some(chunk, carry):
        at = pl.multiple_of(start + chunk * size, size)
        total = held[0] * leaf_ref[0, pl.ds(at, size), :]
        for image in range(1, len(held)):
            total = total + held[image] * leaf_ref[image, pl.ds(at, size), :]
        out_ref[pl.ds(pl.multiple_of(chunk * size, size), size), :] = total
        return carry

    lax.fori_loop(0, out_ref.shape[0] // size, some, 0)


def combine_kernel(unit, gram_ref, leaf_ref, far_ref, own_ref, *message_refs):
    images = leaf_ref.shape[0]
    member, cube, _ = place()
    half = own_ref.shape[0]
    held = tree_factors(jnp.sum(gram_ref[...], 1, keepdims=True), images)
    combine(held, leaf_ref, (1 - cube) * half, far_ref)
    combine(held, leaf_ref, cube * half, own_ref)
    for other, message in zip(EARLY, message_refs):
        pack(member, own_ref, message, other, unit, 0)


def first_unit(target, part):
    low = 2 * part
    return jnp.where(low >= target, 2 * target, jnp.where(low + 1 >= target, 2 * target + 1, 2 * target + 2))


def units(other):
    return 3 if other < 2 else 2


def pack(member, source_ref, message, other, unit, start):
    first = first_unit(member ^ other, member >> 1)
    rows = units(other) * unit
    message[start : start + rows, :] = source_ref[pl.ds(pl.multiple_of(first * unit, unit), rows), :]


def moments_kernel(unit, own_ref, far_ref, *message_refs):
    member, cube, _ = place()
    lower = cube == 0
    own, far = own_ref[...], far_ref[...]
    cross = jnp.sum(own * far, 0, keepdims=True)
    own_sq = jnp.sum(own * own, 0, keepdims=True)
    far_sq = jnp.sum(far * far, 0, keepdims=True)
    lead_sq = jnp.where(lower, own_sq, far_sq)
    second_sq = jnp.where(lower, far_sq, own_sq)
    rest = jnp.zeros((5, own.shape[1]), jnp.float32)
    block = jnp.concatenate([cross, lead_sq, second_sq, rest], 0)
    for other, message in enumerate(message_refs):
        message[0:8, :] = block
        pack(member, far_ref, message, other, unit, 8)
        if other not in EARLY:
            pack(member, own_ref, message, other, unit, 8 + units(other) * unit)


def finish_kernel(unit, images, moments_ref, *refs):
    far, own = refs[:images], refs[images:-2]
    out_ref, placed = refs[-2:]
    member, cube, _ = place()
    lower = cube == 0
    moments = jnp.sum(moments_ref[...], 1, keepdims=True)
    lead, second = factors(moments[0:1], moments[1:2], moments[2:3])
    own_factor = jnp.where(lower, lead, second)
    far_factor = jnp.where(lower, second, lead)
    filters = placed.shape[2]
    for other in range(images):
        rows = units(other) * unit
        own_rows = own[EARLY.index(other)][...] if other in EARLY else far[other][8 + rows :, :]
        placed[member ^ other, 0:rows, :] = own_factor * own_rows + far_factor * far[other][8 : 8 + rows, :]
    for slot in range(images + 1):
        kind = (member + slot) & (images - 1)
        part = kind >> 1
        at = jnp.where(
            part == member >> 1, 0 if slot == 0 else 2 if slot == images else 1, kind & 1
        )
        rows = pl.ds(pl.multiple_of(at * unit, unit), unit)
        for half in range(2):
            out_ref[slot * unit : (slot + 1) * unit, half * filters : (half + 1) * filters] = placed[
                2 * part + half, rows, :
            ]


def exchange(x, other):
    size = lax.axis_size("dp")
    return lax.ppermute(x, "dp", [(i, i ^ other) for i in range(size)])


def swap_cores(x):
    return lax.ppermute(x, "mp", [(0, 1), (1, 0)])


def f32(*shape):
    return jax.ShapeDtypeStruct(shape, jnp.float32)


ORDER = (1, 6, 2, 5, 3, 4, 7)
EARLY = (1, 3, 5, 6)
LAST = (2, 4, 1, 7, 6, 5, 3)
COST = 10**10
BATCHES = ((0, 1, 6), (2, 5), (3, 4), (7,))


def spread(messages):
    received = {0: messages[0]}
    for other in ORDER:
        received[other] = exchange(messages[other], other)
    return received


def local_cube(preact, weights, cotangent):
    extent, own_channels = preact.shape[2], preact.shape[3]
    pixels = preact.shape[1] * preact.shape[2]
    filters, taps, channels = weights.shape
    images = taps - 1
    lanes = own_channels // 4
    unit = channels // lax.axis_size("dp")
    depth = 2 * lanes * taps
    half = depth // 2

    small = pl.CostEstimate(flops=1, bytes_accessed=1, transcendentals=0)

    before = preact.reshape(pixels, own_channels)
    upstream = cotangent.reshape(pixels, filters)
    activity, *sent = pl.pallas_call(
        prepare_kernel,
        in_specs=[VMEM] * 2,
        out_specs=[VMEM] * (1 + images),
        out_shape=[f32(pixels, own_channels)] + [f32(2, pixels, lanes)] * images,
        compiler_params=params(24),
        cost_estimate=small,
        name="prepare",
    )(before, upstream)
    messages = spread(sent)

    leaves, products = None, None
    known = ()
    for batch in BATCHES:
        last = len(known) + len(batch) == images
        size = len(batch)
        if known:
            arrived, leaves = lax.optimization_barrier(([messages[i] for i in batch], leaves))
            messages.update(zip(batch, arrived))
        operands = [messages[i] for i in batch] + [swap_cores(messages[i][0]) for i in batch]
        aliases = {}
        if known:
            aliases = {len(operands) + 1: 0}
            operands += [products, leaves]
        scratch = [
            pltpu.VMEM((size, 2 * lanes, 3 * pixels), jnp.bfloat16),
            pltpu.VMEM((size, 3 * pixels, taps * lanes), jnp.bfloat16),
        ]
        if last:
            scratch.append(pltpu.VMEM((images * images, lanes), jnp.float32))
        leaves, products = pl.pallas_call(
            functools.partial(leaf_kernel, extent, images, known, batch),
            in_specs=[VMEM] * len(operands),
            out_specs=[VMEM, VMEM],
            out_shape=[
                f32(images, depth, lanes),
                f32(-(-len(pairs(images)) // 8) * 8 if last else images * images, lanes),
            ],
            scratch_shapes=scratch,
            input_output_aliases=aliases,
            compiler_params=params(24),
            cost_estimate=small,
        name="leaf",
        )(*operands)
        known += batch
    gram = products
    gram = gram + exchange(gram, 1) + exchange(gram, 2) + exchange(gram, 3)
    gram = gram + exchange(gram, 4)
    gram = gram + swap_cores(gram)

    theirs = swap_cores(activity)
    gram, theirs = lax.optimization_barrier((gram, theirs))
    piece, own, *own_sent = pl.pallas_call(
        functools.partial(combine_kernel, unit),
        in_specs=[VMEM, VMEM],
        out_specs=[VMEM] * (2 + len(EARLY)),
        out_shape=[f32(half, lanes)] * 2 + [f32(units(other) * unit, lanes) for other in EARLY],
        compiler_params=params(24),
        cost_estimate=small,
        name="combine",
    )(gram, leaves)
    far = exchange(piece, images)
    own_messages = [exchange(message, other) for message, other in zip(own_sent, EARLY)]

    activity, piece = lax.optimization_barrier((activity, piece))
    output, kept, given = pl.pallas_call(
        functools.partial(image_kernel, extent),
        grid=(taps,),
        in_specs=[VMEM, VMEM, VMEM, pl.BlockSpec((1, filters, channels), lambda t: (t, 0, 0))],
        out_specs=[VMEM] * 3,
        out_shape=[f32(pixels, filters), f32(pixels, own_channels), f32(pixels, own_channels)],
        scratch_shapes=[
            pltpu.VMEM((pixels + 2 * extent, channels), jnp.bfloat16),
            pltpu.VMEM((pixels + 2 * extent, channels), jnp.bfloat16),
            pltpu.VMEM((3, pixels + 2 * extent, filters), jnp.bfloat16),
            pltpu.VMEM((3, pixels + 2 * extent, filters), jnp.bfloat16),
            pltpu.VMEM((3, pixels, filters), jnp.float32),
            pltpu.VMEM((pixels, channels), jnp.float32),
        ],
        compiler_params=params(44),
        cost_estimate=pl.CostEstimate(flops=COST, bytes_accessed=1, transcendentals=0),
        name="image",
    )(activity, theirs, upstream, weights.transpose(1, 0, 2))
    input_grad = (kept + swap_cores(given)) * gelu_slope(before)

    far, own_messages, output = lax.optimization_barrier((far, own_messages, output))
    far_sent = pl.pallas_call(
        functools.partial(moments_kernel, unit),
        in_specs=[VMEM, VMEM],
        out_specs=[VMEM] * images,
        out_shape=[
            f32(8 + (1 if other in EARLY else 2) * units(other) * unit, lanes) for other in range(images)
        ],
        compiler_params=params(24),
        cost_estimate=small,
        name="moments",
    )(own, far)
    far_messages = {0: far_sent[0]}
    for other in LAST:
        far_messages[other] = exchange(far_sent[other], other)
    moments = far_sent[0][0:8]
    for other in LAST:
        moments, far_messages[other] = lax.optimization_barrier((moments, far_messages[other]))
        moments = moments + far_messages[other][0:8]
    moments = moments + swap_cores(moments)
    moments = moments + exchange(moments, images)
    moments, input_grad = lax.optimization_barrier((moments, input_grad))
    weight_grad = pl.pallas_call(
        functools.partial(finish_kernel, unit, images),
        in_specs=[VMEM] * (1 + images + len(EARLY)),
        out_specs=VMEM,
        out_shape=f32(taps * unit, filters),
        scratch_shapes=[pltpu.VMEM((images, 3 * unit, lanes), jnp.float32)],
        compiler_params=params(24),
        cost_estimate=small,
        name="finish",
    )(moments, *[far_messages[i] for i in range(images)], *own_messages)
    return (
        output.reshape(cotangent.shape),
        input_grad.reshape(preact.shape),
        weight_grad.T,
    )


def local(preact, weights, cotangent):
    count, rows, extent, channels = preact.shape
    filters, taps = weights.shape[:2]
    fits = (
        count == 1
        and taps == 9
        and extent % 16 == 0
        and lax.axis_size("mp") == 2
        and lax.axis_size("dp") == 2 * (taps - 1)
        and channels == 4 * 128
        and filters == 2 * 128
    )
    if fits:
        return local_cube(preact, weights, cotangent)
    return local_any(preact, weights, cotangent)


def solution(mesh):
    in_specs = (P("dp", None, None, "mp"), P("mp", None, None), P("dp", None, None, "mp"))
    out_specs = (P("dp", None, None, "mp"), P("dp", None, None, "mp"), P("mp", "dp"))
    return jax.shard_map(local, mesh=mesh, in_specs=in_specs, out_specs=out_specs, check_vma=False)
```

```python
import functools

import jax
import jax.numpy as jnp
from jax import lax
from jax.experimental import pallas as pl
from jax.experimental.pallas import tpu as pltpu
from jax.sharding import PartitionSpec as P

highest = lax.Precision.HIGHEST
epsilon = 1e-06
MIB = 1 << 20


def from_partner(x, axis, apart):
    return lax.ppermute(x, axis, [(i, i ^ 1 << apart) for i in range(lax.axis_size(axis))])


def activate(values):
    return 0.5 * values * (1.0 + lax.erf(values * 0.7071067811865476))


def gelu_slope(values):
    return (
        0.5 * (1.0 + lax.erf(values * 0.7071067811865476))
        + values * jnp.exp(-0.5 * values * values) * 0.3989422804014327
    )


def pad_image(values):
    return jnp.pad(values, ((0, 0), (1, 1), (1, 1), (0, 0)))


def convolve_piece(activity, filters):
    extent = activity.shape[1]
    padded = pad_image(activity)
    summed = jnp.zeros(activity.shape[:3] + (filters.shape[0],), jnp.float32)
    for kernel_tap in range(9):
        row_shift, column_shift = divmod(kernel_tap, 3)
        window = padded[:, row_shift : row_shift + extent, column_shift : column_shift + extent, :]
        summed = summed + jnp.einsum(
            "nhwc,oc->nhwo", window, filters[:, kernel_tap, :], precision=highest
        )
    return summed


def weight_piece(activity, upstream):
    extent = activity.shape[1]
    padded = pad_image(activity)
    tap_grads = []
    for kernel_tap in range(9):
        row_shift, column_shift = divmod(kernel_tap, 3)
        window = padded[:, row_shift : row_shift + extent, column_shift : column_shift + extent, :]
        tap_grads.append(jnp.einsum("nhwo,nhwc->oc", upstream, window, precision=highest))
    return jnp.stack(tap_grads, 1)


def input_partial(upstream, filters):
    extent = upstream.shape[1]
    padded = pad_image(upstream)
    summed = jnp.zeros(upstream.shape[:3] + (filters.shape[2],), jnp.float32)
    for kernel_tap in range(9):
        row_shift, column_shift = divmod(kernel_tap, 3)
        window = padded[
            :,
            2 - row_shift : 2 - row_shift + extent,
            2 - column_shift : 2 - column_shift + extent,
            :,
        ]
        summed = summed + jnp.einsum(
            "nhwo,oc->nhwc", window, filters[:, kernel_tap, :], precision=highest
        )
    return summed


def adasum_halving(gradient):
    filter_count = gradient.shape[0]
    groups = lax.axis_size("dp")
    height = groups.bit_length() - 1
    data_index = lax.axis_index("dp")
    breadth = gradient.shape[1] * gradient.shape[2] // groups
    current = gradient.reshape(filter_count, groups, breadth)
    for section in range(height):
        parity = data_index >> section & 1
        paired = current.reshape(filter_count, current.shape[1] // 2, 2, breadth)
        kept_rows = lax.dynamic_slice_in_dim(paired, parity, 1, 2)[:, :, 0]
        sent_rows = lax.dynamic_slice_in_dim(paired, 1 - parity, 1, 2)[:, :, 0]
        partner = from_partner(sent_rows, "dp", section)
        lower = parity == 0
        leading = jnp.where(lower, kept_rows, partner)
        second = jnp.where(lower, partner, kept_rows)
        moments = jnp.stack(
            [jnp.sum(leading * second), jnp.sum(leading * leading), jnp.sum(second * second)]
        )
        for bit_level in range(section + 1):
            moments = moments + from_partner(moments, "dp", bit_level)
        moments = lax.psum(moments, "mp")
        cross = moments[0]
        lead_sq = moments[1]
        second_sq = moments[2]
        current = (1.0 - cross / (2.0 * (lead_sq + epsilon))) * leading + (
            1.0 - cross / (2.0 * (second_sq + epsilon))
        ) * second
    return current.reshape(filter_count, breadth)


def local_any(preact, weights, cotangent):
    activity = activate(preact)
    positions = preact.shape[0] * preact.shape[1] * preact.shape[2]
    output = convolve_piece(lax.all_gather(activity, "mp", axis=3, tiled=True), weights)
    gradient = weight_piece(lax.all_gather(activity, "mp", axis=3, tiled=True), cotangent)
    partial_sum = input_partial(cotangent, weights)
    input_grad = lax.psum_scatter(partial_sum, "mp", scatter_dimension=3, tiled=True) * gelu_slope(
        preact
    )
    weight_grad = adasum_halving(gradient / float(positions))
    return (output, input_grad, weight_grad)


VMEM = pl.BlockSpec(memory_space=pltpu.VMEM)


def params(limit):
    return pltpu.CompilerParams(vmem_limit_bytes=limit * MIB)


def split(values):
    high = values.astype(jnp.bfloat16)
    low = (values - high.astype(jnp.float32)).astype(jnp.bfloat16)
    return high, low


def dot(left, right, contract):
    return lax.dot_general(
        left, right, (contract, ((), ())), preferred_element_type=jnp.float32
    )


def dot3(left, right, contract):
    lh, ll = left
    rh, rl = right
    return dot(lh, rh, contract) + (dot(lh, rl, contract) + dot(ll, rh, contract))


def shifted(values, offset, extent):
    if offset == 0:
        return values
    rows = values.shape[0]
    column = lax.rem(lax.broadcasted_iota(jnp.int32, values.shape, 0), extent)
    if offset == 1:
        moved = jnp.concatenate([values[rows - 1 :], values[: rows - 1]], 0)
        return jnp.where(column >= 1, moved, 0.0)
    moved = jnp.concatenate([values[1:], values[:1]], 0)
    return jnp.where(column < extent - 1, moved, 0.0)


def aligned(index, size):
    return pl.ds(pl.multiple_of(index * size, size), size)


def place():
    index = lax.axis_index("dp")
    return index & 7, index >> 3, lax.axis_index("mp")


def prepare_kernel(preact_ref, up_ref, act_ref, *message_refs):
    act_ref[...] = activate(preact_ref[...])
    member = place()[0]
    channels = message_refs[0].shape[2]
    for other, message in enumerate(message_refs):
        target = member ^ other
        message[0] = act_ref[:, aligned(target >> 1, channels)]
        message[1] = up_ref[:, aligned(target & 1, channels)]


def image_kernel(extent, mine_ref, theirs_ref, up_ref, weight_ref,
                 out_ref, keep_ref, send_ref,
                 act_high, act_low, up_high, up_low, total, back):
    step = pl.program_id(0)
    pixels, channels = mine_ref.shape
    core = place()[2]

    @pl.when(step == 0)
    def _():
        for ref in (act_high, act_low):
            ref[...] = jnp.zeros_like(ref)
        for part, at in ((mine_ref, core), (theirs_ref, 1 - core)):
            high, low = split(part[...])
            act_high[extent : extent + pixels, aligned(at, channels)] = high
            act_low[extent : extent + pixels, aligned(at, channels)] = low
        for ref in (up_high, up_low):
            ref[...] = jnp.zeros_like(ref)
        for column in range(3):
            high, low = split(shifted(up_ref[...], column - 1, extent))
            up_high[column, extent : extent + pixels] = high
            up_low[column, extent : extent + pixels] = low
        total[...] = jnp.zeros_like(total)
        back[...] = jnp.zeros_like(back)

    row, column = step // 3, lax.rem(step, 3)
    weight = split(weight_ref[0])
    window = pl.ds(pl.multiple_of(row * extent, extent), pixels)
    total[column] += dot3((act_high[window, :], act_low[window, :]), weight, ((1,), (1,)))
    window = pl.ds(pl.multiple_of((2 - row) * extent, extent), pixels)
    back[...] += dot3((up_high[column, window], up_low[column, window]), weight, ((1,), (0,)))

    @pl.when(step == pl.num_programs(0) - 1)
    def _():
        out_ref[...] = (
            shifted(total[0], 1, extent) + total[1] + shifted(total[2], -1, extent)
        )
        keep_ref[...] = back[:, aligned(core, channels)]
        send_ref[...] = back[:, aligned(1 - core, channels)]


def pairs(count):
    return [(i, j) for i in range(count) for j in range(i, count)]


def leaf_kernel(extent, images, known, others, *refs):
    count = len(others)
    messages, swapped = refs[:count], refs[count : 2 * count]
    refs = refs[2 * count :]
    if known:
        products_in, _ = refs[:2]
        refs = refs[2:]
    leaf, products_ref, left, right = refs[:4]
    pixels, filters = messages[0].shape[1:]
    member, _, core = place()
    scale = 1.0 / pixels
    channels = filters
    depth = 2 * channels

    for at, other in enumerate(others):
        for part, where in ((messages[at][0], core), (swapped[at][...], 1 - core)):
            high, low = split(part.T)
            rows = aligned(where, channels)
            left[at, rows, 0:pixels] = high
            left[at, rows, pixels : 2 * pixels] = high
            left[at, rows, 2 * pixels : 3 * pixels] = low
        for column in range(3):
            moved = shifted(messages[at][1] * scale, column - 1, extent)
            gap = jnp.zeros((extent, filters), jnp.float32)
            for row in range(3):
                if row == 0:
                    placed = jnp.concatenate([moved[extent:], gap], 0)
                elif row == 2:
                    placed = jnp.concatenate([gap, moved[: pixels - extent]], 0)
                else:
                    placed = moved
                high, low = split(placed)
                tap = 3 * row + column
                lanes = slice(tap * filters, (tap + 1) * filters)
                right[at, 0:pixels, lanes] = high
                right[at, pixels : 2 * pixels, lanes] = low
                right[at, 2 * pixels : 3 * pixels, lanes] = high
        product = dot(left[at], right[at], ((1,), (0,)))
        image = member ^ other
        for tap in range(9):
            leaf[image, tap * depth : (tap + 1) * depth, :] = product[
                :, tap * filters : (tap + 1) * filters
            ]

    fresh = [(i, j) for at, i in enumerate(others) for j in list(known) + list(others[: at + 1])]
    held = list(known) + list(others)

    def add(chunk, sums):
        rows = pl.ds(pl.multiple_of(chunk * 8, 8), 8)
        blocks = {i: leaf[member ^ i, rows, :] for i in held}
        return tuple(s + blocks[i] * blocks[j] for s, (i, j) in zip(sums, fresh))

    zero = jnp.zeros((8, filters), jnp.float32)
    sums = lax.fori_loop(0, leaf.shape[1] // 8, add, tuple(zero for _ in fresh), unroll=4)
    table = products_ref if len(held) < images else refs[4]
    if known:
        table[...] = products_in[...]
    else:
        table[...] = jnp.zeros_like(table)
    for block, (i, j) in zip(sums, fresh):
        line = jnp.sum(block, 0, keepdims=True)
        table[i * images + j : i * images + j + 1, :] = line
        table[j * images + i : j * images + i + 1, :] = line
    if len(held) == images:
        products_ref[...] = jnp.zeros_like(products_ref)
        for at, (i, j) in enumerate(pairs(images)):
            products_ref[at : at + 1, :] = table[pl.ds((member ^ i) * images + (member ^ j), 1), :]


def factors(cross, lead_sq, second_sq):
    return (
        1.0 - cross / (2.0 * (lead_sq + epsilon)),
        1.0 - cross / (2.0 * (second_sq + epsilon)),
    )


def tree_factors(gram, images):
    inner = {pair: gram[at : at + 1, :] for at, pair in enumerate(pairs(images))}
    held = [1.0] * images
    count, width = images, 1
    while count > 1:
        scaled = []
        for node in range(0, count, 2):
            scaled += factors(
                inner[node, node + 1],
                jnp.maximum(inner[node, node], 0.0),
                jnp.maximum(inner[node + 1, node + 1], 0.0),
            )
        held = [value * scaled[at // width] for at, value in enumerate(held)]
        merged = {}
        for i, j in pairs(count // 2):
            terms = [
                scaled[2 * i + u] * scaled[2 * j + v] * inner[min(2 * i + u, 2 * j + v), max(2 * i + u, 2 * j + v)]
                for u in range(2)
                for v in range(2)
            ]
            merged[i, j] = (terms[0] + terms[1]) + (terms[2] + terms[3])
        inner, count, width = merged, count // 2, 2 * width
    return held


def combine(held, leaf_ref, start, out_ref):
    size = 64

    def some(chunk, carry):
        at = pl.multiple_of(start + chunk * size, size)
        total = held[0] * leaf_ref[0, pl.ds(at, size), :]
        for image in range(1, len(held)):
            total = total + held[image] * leaf_ref[image, pl.ds(at, size), :]
        out_ref[pl.ds(pl.multiple_of(chunk * size, size), size), :] = total
        return carry

    lax.fori_loop(0, out_ref.shape[0] // size, some, 0)


def combine_kernel(unit, gram_ref, leaf_ref, far_ref, own_ref, *message_refs):
    images = leaf_ref.shape[0]
    member, cube, _ = place()
    half = own_ref.shape[0]
    held = tree_factors(jnp.sum(gram_ref[...], 1, keepdims=True), images)
    combine(held, leaf_ref, (1 - cube) * half, far_ref)
    combine(held, leaf_ref, cube * half, own_ref)
    for other, message in zip(EARLY, message_refs):
        pack(member, own_ref, message, other, unit, 0)


def first_unit(target, part):
    low = 2 * part
    return jnp.where(low >= target, 2 * target, jnp.where(low + 1 >= target, 2 * target + 1, 2 * target + 2))


def units(other):
    return 3 if other < 2 else 2


def pack(member, source_ref, message, other, unit, start):
    first = first_unit(member ^ other, member >> 1)
    rows = units(other) * unit
    message[start : start + rows, :] = source_ref[pl.ds(pl.multiple_of(first * unit, unit), rows), :]


def moments_kernel(unit, own_ref, far_ref, *message_refs):
    member, cube, _ = place()
    lower = cube == 0
    own, far = own_ref[...], far_ref[...]
    cross = jnp.sum(own * far, 0, keepdims=True)
    own_sq = jnp.sum(own * own, 0, keepdims=True)
    far_sq = jnp.sum(far * far, 0, keepdims=True)
    lead_sq = jnp.where(lower, own_sq, far_sq)
    second_sq = jnp.where(lower, far_sq, own_sq)
    rest = jnp.zeros((5, own.shape[1]), jnp.float32)
    block = jnp.concatenate([cross, lead_sq, second_sq, rest], 0)
    for other, message in enumerate(message_refs):
        message[0:8, :] = block
        pack(member, far_ref, message, other, unit, 8)
        if other not in EARLY:
            pack(member, own_ref, message, other, unit, 8 + units(other) * unit)


def finish_kernel(unit, images, moments_ref, *refs):
    far, own = refs[:images], refs[images:-4]
    out_ref, placed, joined, sems = refs[-4:]
    member, cube, _ = place()
    lower = cube == 0
    moments = jnp.sum(moments_ref[...], 1, keepdims=True)
    lead, second = factors(moments[0:1], moments[1:2], moments[2:3])
    own_factor = jnp.where(lower, lead, second)
    far_factor = jnp.where(lower, second, lead)
    filters = placed.shape[2]
    for other in range(images):
        rows = units(other) * unit
        own_rows = own[EARLY.index(other)][...] if other in EARLY else far[other][8 + rows :, :]
        placed[member ^ other, 0:rows, :] = own_factor * own_rows + far_factor * far[other][8 : 8 + rows, :]
    copies = []
    for slot in range(images + 1):
        kind = (member + slot) & (images - 1)
        part = kind >> 1
        at = jnp.where(
            part == member >> 1, 0 if slot == 0 else 2 if slot == images else 1, kind & 1
        )
        rows = pl.ds(pl.multiple_of(at * unit, unit), unit)
        mine = slice(slot * unit, (slot + 1) * unit)
        for half in range(2):
            joined[mine, half * filters : (half + 1) * filters] = placed[2 * part + half, rows, :]
        if slot % 3 == 2:
            mine = slice((slot - 2) * unit, (slot + 1) * unit)
            copies.append(pltpu.make_async_copy(joined.at[mine], out_ref.at[mine], sems.at[slot // 3]))
            copies[-1].start()
    for copy in copies:
        copy.wait()


def exchange(x, other):
    size = lax.axis_size("dp")
    return lax.ppermute(x, "dp", [(i, i ^ other) for i in range(size)])


def swap_cores(x):
    return lax.ppermute(x, "mp", [(0, 1), (1, 0)])


def f32(*shape):
    return jax.ShapeDtypeStruct(shape, jnp.float32)


ORDER = (1, 6, 2, 5, 3, 4, 7)
EARLY = (1, 3, 5, 6)
LAST = (2, 4, 1, 7, 6, 5, 3)
COST = 10**10
BATCHES = ((0, 1, 6), (2, 5), (3, 4), (7,))


def spread(messages):
    received = {0: messages[0]}
    for other in ORDER:
        received[other] = exchange(messages[other], other)
    return received


def local_cube(preact, weights, cotangent):
    extent, own_channels = preact.shape[2], preact.shape[3]
    pixels = preact.shape[1] * preact.shape[2]
    filters, taps, channels = weights.shape
    images = taps - 1
    lanes = own_channels // 4
    unit = channels // lax.axis_size("dp")
    depth = 2 * lanes * taps
    half = depth // 2

    small = pl.CostEstimate(flops=1, bytes_accessed=1, transcendentals=0)

    before = preact.reshape(pixels, own_channels)
    upstream = cotangent.reshape(pixels, filters)
    activity, *sent = pl.pallas_call(
        prepare_kernel,
        in_specs=[VMEM] * 2,
        out_specs=[VMEM] * (1 + images),
        out_shape=[f32(pixels, own_channels)] + [f32(2, pixels, lanes)] * images,
        compiler_params=params(24),
        cost_estimate=small,
        name="prepare",
    )(before, upstream)
    messages = spread(sent)

    leaves, products = None, None
    known = ()
    for batch in BATCHES:
        last = len(known) + len(batch) == images
        size = len(batch)
        if known:
            arrived, leaves = lax.optimization_barrier(([messages[i] for i in batch], leaves))
            messages.update(zip(batch, arrived))
        operands = [messages[i] for i in batch] + [swap_cores(messages[i][0]) for i in batch]
        aliases = {}
        if known:
            aliases = {len(operands) + 1: 0}
            operands += [products, leaves]
        scratch = [
            pltpu.VMEM((size, 2 * lanes, 3 * pixels), jnp.bfloat16),
            pltpu.VMEM((size, 3 * pixels, taps * lanes), jnp.bfloat16),
        ]
        if last:
            scratch.append(pltpu.VMEM((images * images, lanes), jnp.float32))
        leaves, products = pl.pallas_call(
            functools.partial(leaf_kernel, extent, images, known, batch),
            in_specs=[VMEM] * len(operands),
            out_specs=[VMEM, VMEM],
            out_shape=[
                f32(images, depth, lanes),
                f32(-(-len(pairs(images)) // 8) * 8 if last else images * images, lanes),
            ],
            scratch_shapes=scratch,
            input_output_aliases=aliases,
            compiler_params=params(24),
            cost_estimate=small,
        name="leaf",
        )(*operands)
        known += batch
    gram = products
    gram = gram + exchange(gram, 1) + exchange(gram, 2) + exchange(gram, 3)
    gram = gram + exchange(gram, 4)
    gram = gram + swap_cores(gram)

    theirs = swap_cores(activity)
    gram, theirs = lax.optimization_barrier((gram, theirs))
    piece, own, *own_sent = pl.pallas_call(
        functools.partial(combine_kernel, unit),
        in_specs=[VMEM, VMEM],
        out_specs=[VMEM] * (2 + len(EARLY)),
        out_shape=[f32(half, lanes)] * 2 + [f32(units(other) * unit, lanes) for other in EARLY],
        compiler_params=params(24),
        cost_estimate=small,
        name="combine",
    )(gram, leaves)
    far = exchange(piece, images)
    own_messages = [exchange(message, other) for message, other in zip(own_sent, EARLY)]

    activity, piece = lax.optimization_barrier((activity, piece))
    output, kept, given = pl.pallas_call(
        functools.partial(image_kernel, extent),
        grid=(taps,),
        in_specs=[VMEM, VMEM, VMEM, pl.BlockSpec((1, filters, channels), lambda t: (t, 0, 0))],
        out_specs=[VMEM] * 3,
        out_shape=[f32(pixels, filters), f32(pixels, own_channels), f32(pixels, own_channels)],
        scratch_shapes=[
            pltpu.VMEM((pixels + 2 * extent, channels), jnp.bfloat16),
            pltpu.VMEM((pixels + 2 * extent, channels), jnp.bfloat16),
            pltpu.VMEM((3, pixels + 2 * extent, filters), jnp.bfloat16),
            pltpu.VMEM((3, pixels + 2 * extent, filters), jnp.bfloat16),
            pltpu.VMEM((3, pixels, filters), jnp.float32),
            pltpu.VMEM((pixels, channels), jnp.float32),
        ],
        compiler_params=params(44),
        cost_estimate=pl.CostEstimate(flops=COST, bytes_accessed=1, transcendentals=0),
        name="image",
    )(activity, theirs, upstream, weights.transpose(1, 0, 2))
    input_grad = (kept + swap_cores(given)) * gelu_slope(before)

    far, own_messages, output = lax.optimization_barrier((far, own_messages, output))
    far_sent = pl.pallas_call(
        functools.partial(moments_kernel, unit),
        in_specs=[VMEM, VMEM],
        out_specs=[VMEM] * images,
        out_shape=[
            f32(8 + (1 if other in EARLY else 2) * units(other) * unit, lanes) for other in range(images)
        ],
        compiler_params=params(24),
        cost_estimate=small,
        name="moments",
    )(own, far)
    far_messages = {0: far_sent[0]}
    for other in LAST:
        far_messages[other] = exchange(far_sent[other], other)
    moments = far_sent[0][0:8]
    for other in LAST:
        moments, far_messages[other] = lax.optimization_barrier((moments, far_messages[other]))
        moments = moments + far_messages[other][0:8]
    moments = moments + swap_cores(moments)
    moments = moments + exchange(moments, images)
    moments, input_grad = lax.optimization_barrier((moments, input_grad))
    weight_grad = pl.pallas_call(
        functools.partial(finish_kernel, unit, images),
        in_specs=[VMEM] * (1 + images + len(EARLY)),
        out_specs=pl.BlockSpec(memory_space=pl.ANY),
        out_shape=f32(taps * unit, filters),
        scratch_shapes=[
            pltpu.VMEM((images, 3 * unit, lanes), jnp.float32),
            pltpu.VMEM((taps * unit, filters), jnp.float32),
            pltpu.SemaphoreType.DMA((3,)),
        ],
        compiler_params=params(24),
        cost_estimate=small,
        name="finish",
    )(moments, *[far_messages[i] for i in range(images)], *own_messages)
    return (
        output.reshape(cotangent.shape),
        input_grad.reshape(preact.shape),
        weight_grad.T,
    )


def local(preact, weights, cotangent):
    count, rows, extent, channels = preact.shape
    filters, taps = weights.shape[:2]
    fits = (
        count == 1
        and taps == 9
        and extent % 16 == 0
        and lax.axis_size("mp") == 2
        and lax.axis_size("dp") == 2 * (taps - 1)
        and channels == 4 * 128
        and filters == 2 * 128
    )
    if fits:
        return local_cube(preact, weights, cotangent)
    return local_any(preact, weights, cotangent)


def solution(mesh):
    in_specs = (P("dp", None, None, "mp"), P("mp", None, None), P("dp", None, None, "mp"))
    out_specs = (P("dp", None, None, "mp"), P("dp", None, None, "mp"), P("mp", "dp"))
    return jax.shard_map(local, mesh=mesh, in_specs=in_specs, out_specs=out_specs, check_vma=False)
```
